256 devices in a mesh: seq: 64 (over z, y, core), res: 4 (over x).
Axes of the slice: x: 4, y: 4, z: 8, core: 2. Of those that a mesh axis runs over, the one named last changes fastest.
Arguments:
- alignment_embedding: bfloat16 [256, 512, 768], P('seq', 'res'), may hold values from -6 to 6
- horizontal_scaling_factor: float32 [768], replicated, may hold values from 0.25 to 1.75
- horizontal_asking_matrix: bfloat16 [768, 768], replicated, may hold values from -4 to 4
- horizontal_lookup_matrix: bfloat16 [768, 768], replicated, may hold values from -4 to 4
- horizontal_content_matrix: bfloat16 [768, 768], replicated, may hold values from -0.21875 to 0.21875
- horizontal_mixing_matrix: bfloat16 [768, 768], replicated, may hold values from -0.21875 to 0.21875
- vertical_scaling_factor: float32 [768], replicated, may hold values from 0.25 to 1.75
- vertical_asking_matrix: bfloat16 [768, 768], replicated, may hold values from -4 to 4
- vertical_lookup_matrix: bfloat16 [768, 768], replicated, may hold values from -4 to 4
- vertical_content_matrix: bfloat16 [768, 768], replicated, may hold values from -0.21875 to 0.21875
- vertical_mixing_matrix: bfloat16 [768, 768], replicated, may hold values from -0.21875 to 0.21875
Outputs:
- result: bfloat16 [256, 512, 768], P('seq', 'res')
The draws below stay inside these ranges and needn't reach their ends.
All inputs are finite; a program needn't handle non-finite values.
Results may differ from the reference program's by a relative error of at most 0.009.
Values may be sent and summed in bfloat16 or wider, within the bound.
A program may use at most 64 MiB of HBM per device.

```python
import math
import jax
import jax.numpy as jnp
from jax import lax

EMBED_DIMENSION = 768
HEADS = 12
ALIGNED_CHAINS = 256
ALIGNED_SITES = 512


def base_matrix(key, salt):
    return jax.random.normal(jax.random.fold_in(key, salt), (EMBED_DIMENSION, EMBED_DIMENSION), jnp.float32) * EMBED_DIMENSION ** (-0.5)


def draw_horizontal_lookup_matrix(key, part):
    shared = base_matrix(key, 101)
    return shared.astype(jnp.bfloat16)


def draw_horizontal_asking_matrix(key, part):
    key = jax.random.fold_in(key, 2)
    fresh = jax.random.normal(key, (EMBED_DIMENSION, EMBED_DIMENSION), jnp.float32) * EMBED_DIMENSION ** (-0.5)
    return fresh.astype(jnp.bfloat16)


def draw_vertical_lookup_matrix(key, part):
    shared = base_matrix(key, 202)
    return shared.astype(jnp.bfloat16)


def draw_vertical_asking_matrix(key, part):
    key = jax.random.fold_in(key, 4)
    fresh = jax.random.normal(key, (EMBED_DIMENSION, EMBED_DIMENSION), jnp.float32) * EMBED_DIMENSION ** (-0.5)
    return fresh.astype(jnp.bfloat16)


def level_of(key, extent, shards, least, high):
    def one(position, blocks):
        heights = jax.random.uniform(jax.random.fold_in(jax.random.fold_in(key, 6), position), (blocks,), jnp.float32, least / len(shards), high / len(shards))
        return jnp.repeat(jnp.exp(heights), extent[position] // blocks).reshape((-1,) + (1,) * (len(extent) - position - 1))

    level = one(*shards[0])
    for cut in shards[1:]:
        level = level * one(*cut)
    return level


def scatter_about(own_key, shape, scale, limit, cuts=(), kind=jnp.bfloat16):
    entries = jax.random.normal(own_key, shape, jnp.float32) * scale
    if len(cuts) > 0:
        entries = level_of(own_key, shape, cuts, -0.22, 0.18) * entries
    return jnp.clip(entries, min=-limit, max=limit).astype(kind)


def setup_inputs(seed: int = 0) -> dict:
    key_list = jax.random.split(jax.random.key(seed), 12)
    alignment_embedding = scatter_about(key_list[0], (ALIGNED_CHAINS, ALIGNED_SITES, EMBED_DIMENSION), 1.0, 6.0, ((0, 64), (1, 4)))
    horizontal_scaling_factor = jnp.clip(1.0 + 0.15 * jax.random.normal(key_list[1], (EMBED_DIMENSION,), jnp.float32), 0.25, 1.75)
    horizontal_asking_matrix = draw_horizontal_asking_matrix(jax.random.fold_in(key_list[11], 71), 0)
    horizontal_lookup_matrix = draw_horizontal_lookup_matrix(jax.random.fold_in(key_list[11], 71), 0)
    horizontal_content_matrix = scatter_about(key_list[4], (EMBED_DIMENSION, EMBED_DIMENSION), EMBED_DIMENSION ** -0.5, 0.21875)
    horizontal_mixing_matrix = scatter_about(key_list[5], (EMBED_DIMENSION, EMBED_DIMENSION), EMBED_DIMENSION ** -0.5, 0.21875)
    vertical_scaling_factor = jnp.clip(1.0 + 0.15 * jax.random.normal(key_list[6], (EMBED_DIMENSION,), jnp.float32), 0.25, 1.75)
    vertical_asking_matrix = draw_vertical_asking_matrix(jax.random.fold_in(key_list[11], 71), 0)
    vertical_lookup_matrix = draw_vertical_lookup_matrix(jax.random.fold_in(key_list[11], 71), 0)
    vertical_content_matrix = scatter_about(key_list[9], (EMBED_DIMENSION, EMBED_DIMENSION), EMBED_DIMENSION ** -0.5, 0.21875)
    vertical_mixing_matrix = scatter_about(key_list[10], (EMBED_DIMENSION, EMBED_DIMENSION), EMBED_DIMENSION ** -0.5, 0.21875)
    return {"alignment_embedding": alignment_embedding, "horizontal_scaling_factor": horizontal_scaling_factor, "horizontal_asking_matrix": horizontal_asking_matrix, "horizontal_lookup_matrix": horizontal_lookup_matrix, "horizontal_content_matrix": horizontal_content_matrix, "horizontal_mixing_matrix": horizontal_mixing_matrix, "vertical_scaling_factor": vertical_scaling_factor, "vertical_asking_matrix": vertical_asking_matrix, "vertical_lookup_matrix": vertical_lookup_matrix, "vertical_content_matrix": vertical_content_matrix, "vertical_mixing_matrix": vertical_mixing_matrix}


def standardize_activations(values, gain):
    wide = values.astype(jnp.float32)
    center = wide - lax.optimization_barrier(jnp.mean(wide, axis=-1, keepdims=True))
    spread = lax.optimization_barrier(jnp.mean(center * center, axis=-1, keepdims=True))
    return (center * lax.rsqrt(spread + 1e-05) * gain.astype(jnp.float32)).astype(jnp.bfloat16)

def project(standardized_hidden, weight):
    return jnp.dot(standardized_hidden.reshape(-1, EMBED_DIMENSION), weight, preferred_element_type=jnp.float32).astype(jnp.bfloat16)

def column_one(items):
    col_q, col_k, col_v = items
    embedding_dimension = col_q.shape[-1]
    scores = jnp.einsum('she,the->hst', col_q.astype(jnp.float32), col_k.astype(jnp.float32)) * (1.0 / math.sqrt(embedding_dimension))
    probs = jax.nn.softmax(scores, axis=-1).astype(jnp.bfloat16)
    return jnp.einsum('hst,the->she', probs.astype(jnp.float32), col_v.astype(jnp.float32)).astype(jnp.bfloat16)

def reference(alignment_embedding, horizontal_scaling_factor, horizontal_asking_matrix, horizontal_lookup_matrix, horizontal_content_matrix, horizontal_mixing_matrix, vertical_scaling_factor, vertical_asking_matrix, vertical_lookup_matrix, vertical_content_matrix, vertical_mixing_matrix):
    embedding_dimension = EMBED_DIMENSION // HEADS
    standardized_hidden = standardize_activations(alignment_embedding, horizontal_scaling_factor)
    row_q = project(standardized_hidden, horizontal_asking_matrix).reshape(ALIGNED_CHAINS, ALIGNED_SITES, HEADS, embedding_dimension)
    row_k = project(standardized_hidden, horizontal_lookup_matrix).reshape(ALIGNED_CHAINS, ALIGNED_SITES, HEADS, embedding_dimension)
    row_v = project(standardized_hidden, horizontal_content_matrix).reshape(ALIGNED_CHAINS, ALIGNED_SITES, HEADS, embedding_dimension)
    tied = jnp.einsum('sihe,sjhe->hij', row_q.astype(jnp.float32), row_k.astype(jnp.float32))
    tied = tied * (1.0 / (math.sqrt(embedding_dimension) * math.sqrt(ALIGNED_CHAINS)))
    row_prob = jax.nn.softmax(tied, axis=-1).astype(jnp.bfloat16)
    row_attended = jnp.einsum('hij,sjhe->sihe', row_prob.astype(jnp.float32), row_v.astype(jnp.float32)).astype(jnp.bfloat16)
    residual_increment = jnp.dot(row_attended.reshape(-1, EMBED_DIMENSION), horizontal_mixing_matrix, preferred_element_type=jnp.float32).reshape(ALIGNED_CHAINS, ALIGNED_SITES, EMBED_DIMENSION)
    hidden_post_horizontal = (alignment_embedding.astype(jnp.float32) + residual_increment).astype(jnp.bfloat16)
    col_normed = standardize_activations(hidden_post_horizontal, vertical_scaling_factor)
    col_q = jnp.moveaxis(project(col_normed, vertical_asking_matrix).reshape(ALIGNED_CHAINS, ALIGNED_SITES, HEADS, embedding_dimension), 1, 0)
    col_k = jnp.moveaxis(project(col_normed, vertical_lookup_matrix).reshape(ALIGNED_CHAINS, ALIGNED_SITES, HEADS, embedding_dimension), 1, 0)
    col_v = jnp.moveaxis(project(col_normed, vertical_content_matrix).reshape(ALIGNED_CHAINS, ALIGNED_SITES, HEADS, embedding_dimension), 1, 0)
    col_mixed = jnp.moveaxis(lax.map(column_one, (col_q, col_k, col_v)), 0, 1)
    residual_increment = jnp.dot(col_mixed.reshape(-1, EMBED_DIMENSION), vertical_mixing_matrix, preferred_element_type=jnp.float32).reshape(ALIGNED_CHAINS, ALIGNED_SITES, EMBED_DIMENSION)
    return (hidden_post_horizontal.astype(jnp.float32) + residual_increment).astype(jnp.bfloat16)
```

```python
import functools
import math

import jax
import jax.numpy as jnp
from jax import lax
from jax.experimental import pallas as pl
from jax.experimental.pallas import tpu as pltpu
from jax.sharding import PartitionSpec as P

MESH = pl.DeviceIdType.MESH
HEADS = 12
HEAD = 64
WIDTH = HEADS * HEAD
LANES = 128
SLABS = WIDTH // LANES
BF = jnp.bfloat16
F32 = jnp.float32
NT = (((1,), (1,)), ((), ()))


class Dims:
    def __init__(self, nseq, nx, ny, chains, sites):
        self.nx, self.ny, self.nc = nx, ny, 2
        self.nz = nseq // (2 * ny)
        self.nd = self.ny * self.nz
        self.chains, self.sites = chains, sites
        self.rows = chains * sites
        self.hx = HEADS // nx
        self.total_sites = sites * nx
        self.half = self.total_sites // 2
        self.yrows = self.half // ny
        self.zrows = self.yrows // self.nz
        self.zpad = -(-(self.hx * self.zrows) // 16) * 16
        self.csites = sites // 2
        self.pair = 2 * chains
        self.cols = self.csites // self.nd
        self.drows = self.cols * self.pair
        self.col_len = self.nd * self.pair
        self.total_seqs = nseq * chains


def normed(wide, gain):
    center = wide - jnp.mean(wide, axis=-1, keepdims=True)
    spread = jnp.mean(center * center, axis=-1, keepdims=True)
    return (center * lax.rsqrt(spread + 1e-05) * gain).astype(BF)


def softmax(scores):
    top = jnp.max(scores, axis=-1, keepdims=True)
    e = jnp.exp(scores - top)
    return (e / jnp.sum(e, axis=-1, keepdims=True)).astype(BF)


def layer(
    D,
    a_ref, g1_ref, g2_ref,
    wq, wk, wv, wo, cq, ck, cv, co,
    out_ref,
    w_buf, xn, qkv_s, qkv_r, l_own, l_send, l_recv, y_send, y_recv, z_sum, z_send, z_recv,
    p_send, p_z, p_full, o_send, m_recv, a_res, mix, c_f32, c_send, c_recv, cn, c_qkv, c_mix,
    r_send, r_recv, f_send,
    w_sem, x_ss, x_rs, x_ls, a_sem, c_ss, c_rs, y_ss, y_rs, z_ss, z_rs, pz_ss, pz_rs, py_ss, py_rs,
    pc_sem, o_ss, o_rs, o_ls, i_ss, i_rs, i_ls, b_ss, b_rs, b_ls, f_sem,
):
    nx, ny, nz, nd, hx = D.nx, D.ny, D.nz, D.nd, D.hx
    seq, x = lax.axis_index("seq"), lax.axis_index("res")
    c = lax.rem(seq, 2)
    d = seq // 2
    y = lax.rem(d, ny)
    z = d // ny
    other = 1 - c

    def dev(z_, y_, c_, x_):
        return ((z_ * ny + y_) * 2 + c_, x_)

    sibling = dev(z, y, other, x)

    def remote(src, dst, ss, rs, to):
        return pltpu.make_async_remote_copy(
            src_ref=src, dst_ref=dst, send_sem=ss, recv_sem=rs, device_id=to, device_id_type=MESH
        )

    def loop(lo, hi, body):
        def step(k, carry):
            body(k)
            return carry

        lax.fori_loop(lo, hi, step, 0)

    def drain(ref, *sems):
        for sem in sems:
            pltpu.make_async_copy(ref, ref, sem).wait()

    weights = (wq, wk, wv, wo, cq, ck, cv, co)
    w_copies = [pltpu.make_async_copy(w, w_buf.at[n], w_sem.at[n]) for n, w in enumerate(weights)]
    for copy in w_copies:
        copy.start()

    bar = pltpu.get_barrier_semaphore()

    def greet(to):
        pl.semaphore_signal(bar, inc=1, device_id=to, device_id_type=MESH)

    def x_core(k):
        g = lax.rem(x * 2 + c + k, 2 * nx)
        return g // 2, lax.rem(g, 2)

    def greet_d(k):
        p = lax.rem(d + k, nd)
        greet(dev(p // ny, lax.rem(p, ny), c, x))

    def greet_x(k):
        xo, co_ = x_core(k)
        greet(dev(z, y, co_, xo))

    loop(1, nd, greet_d)
    loop(1, 2 * nx, greet_x)

    def norm_rows(s):
        xn[pl.ds(pl.multiple_of(s * D.sites, D.sites), D.sites), :] = normed(
            a_ref[s].astype(F32), g1_ref[...]
        )

    loop(0, D.chains, norm_rows)
    pl.semaphore_wait(bar, nd - 1 + 2 * nx - 1)

    a_half = pl.ds(pl.multiple_of(c * D.csites, D.csites), D.csites)
    a_other = pl.ds(pl.multiple_of(other * D.csites, D.csites), D.csites)
    a_local = pltpu.make_async_copy(a_ref.at[:, a_half, :], a_res.at[c], a_sem.at[0])
    a_local.start()
    a_copy = remote(a_ref.at[:, a_other, :], a_res.at[c], a_sem.at[1], a_sem.at[2], sibling)
    a_copy.start()

    my_sites = pl.ds(pl.multiple_of(x * D.sites, D.sites), D.sites)

    def x_copy(m, k):
        xo = lax.rem(x + k, nx)
        return remote(
            qkv_s.at[m, pl.ds(xo * hx, hx)], qkv_r.at[m, :, my_sites, :], x_ss.at[m], x_rs.at[m], dev(z, y, c, xo)
        )

    def x_local(m):
        return pltpu.make_async_copy(
            qkv_s.at[m, pl.ds(x * hx, hx)], qkv_r.at[m, :, my_sites, :], x_ls.at[m]
        )

    for m in range(3):
        w_copies[m].wait()

        def project(cb, m=m):
            cols = pl.ds(pl.multiple_of(cb * 256, 256), 256)
            t = jnp.dot(xn[...], w_buf[m, :, cols], preferred_element_type=F32).astype(BF)
            for hh in range(4):
                qkv_s[m, cb * 4 + hh] = jnp.concatenate(
                    [
                        t[s * D.sites : (s + 1) * D.sites, hh * HEAD : (hh + 1) * HEAD]
                        for s in range(D.chains)
                    ],
                    axis=-1,
                )

        loop(0, WIDTH // 256, project)
        x_local(m).start()
        loop(1, nx, lambda k, m=m: x_copy(m, k).start())

    def x_wait(m):
        x_local(m).wait()
        drain(qkv_r.at[m, :, pl.ds(0, (nx - 1) * D.sites), :], x_ss.at[m], x_rs.at[m])

    x_wait(0)
    x_wait(1)

    scale = 1.0 / (math.sqrt(HEAD) * math.sqrt(D.total_seqs))
    own_half = pl.ds(pl.multiple_of(c * D.half, D.half), D.half)
    far_half = pl.ds(pl.multiple_of(other * D.half, D.half), D.half)

    def c_copy(h):
        return remote(l_send.at[h], l_recv.at[h], c_ss.at[h], c_rs.at[h], sibling)

    def logits(h):
        keys = qkv_r[1, h]
        far = lax.dot_general(qkv_r[0, h, far_half, :], keys, NT, preferred_element_type=F32)
        l_send[h] = (far * scale).astype(BF)
        c_copy(h).start()
        own = lax.dot_general(qkv_r[0, h, own_half, :], keys, NT, preferred_element_type=F32)
        l_own[h] = own * scale

    loop(0, hx, logits)

    def y_rows(i):
        return pl.ds(pl.multiple_of(i * D.yrows, D.yrows), D.yrows)

    def y_copy(h, k):
        yo = lax.rem(y + k, ny)
        return remote(
            y_send.at[h, y_rows(yo), :], y_recv.at[y, h], y_ss.at[h], y_rs.at[h], dev(z, yo, c, x)
        )

    def core_sum(h):
        c_copy(h).wait()
        total = l_own[h] + l_recv[h].astype(F32)
        l_own[h] = total
        y_send[h] = total.astype(BF)
        loop(1, ny, lambda k: y_copy(h, k).start())

    loop(0, hx, core_sum)

    def y_sum(h):
        drain(y_recv.at[pl.ds(0, ny - 1), h], y_ss.at[h], y_rs.at[h])
        z_sum[h] = l_own[h, y_rows(y), :]

        def add(k):
            z_sum[h] += y_recv[lax.rem(y + k, ny), h].astype(F32)

        loop(1, ny, add)

    loop(0, hx, y_sum)

    zr = hx * D.zrows

    def z_fill(i):
        rows = pl.ds(pl.multiple_of(i * D.zrows, D.zrows), D.zrows)
        part = [z_sum[h, rows, :] for h in range(hx)]
        if D.zpad > zr:
            part.append(jnp.zeros((D.zpad - zr, D.total_sites), F32))
        z_send[i] = jnp.concatenate(part, axis=0).astype(BF)

    loop(0, nz, z_fill)

    def z_copy(k):
        zo = lax.rem(z + k, nz)
        return remote(z_send.at[zo], z_recv.at[z], z_ss, z_rs, dev(zo, y, c, x))

    loop(1, nz, lambda k: z_copy(k).start())
    drain(z_recv.at[pl.ds(0, nz - 1)], z_ss, z_rs)

    def z_add(k, total):
        return total + z_recv[lax.rem(z + k, nz)].astype(F32)

    tied = lax.fori_loop(1, nz, z_add, z_send[z].astype(F32))
    p_send[...] = softmax(tied)

    def pz_copy(k):
        zo = lax.rem(z + k, nz)
        return remote(p_send, p_z.at[z], pz_ss, pz_rs, dev(zo, y, c, x))

    loop(1, nz, lambda k: pz_copy(k).start())
    p_z[z] = p_send[...]
    drain(p_z.at[pl.ds(0, nz - 1)], pz_ss, pz_rs)

    def p_fill(i):
        rows = pl.ds(pl.multiple_of(i * D.zrows, D.zrows), D.zrows)
        block = p_z[i].astype(F32)
        for h in range(hx):
            z_sum[h, rows, :] = block[h * D.zrows : (h + 1) * D.zrows]

    loop(0, nz, p_fill)
    py_rows = pl.ds(pl.multiple_of(c * D.half + y * D.yrows, D.yrows), D.yrows)
    p_full[:, py_rows, :] = z_sum[...].astype(BF)

    def py_copy(k):
        yo = lax.rem(y + k, ny)
        return remote(
            p_full.at[:, py_rows, :], p_full.at[:, py_rows, :], py_ss, py_rs, dev(z, yo, c, x)
        )

    loop(1, ny, lambda k: py_copy(k).start())
    drain(p_full.at[:, pl.ds(0, (ny - 1) * D.yrows), :], py_ss, py_rs)
    pc_copy = remote(
        p_full.at[:, own_half, :], p_full.at[:, own_half, :], pc_sem.at[0], pc_sem.at[1], sibling
    )
    pc_copy.start()
    x_wait(2)
    pc_copy.wait()

    def o_rows(xo, co_):
        return pl.ds(pl.multiple_of(xo * D.sites + co_ * D.csites, D.csites), D.csites)

    def o_copy(h, k):
        xo, co_ = x_core(k)
        return remote(
            o_send.at[h, o_rows(xo, co_), :], m_recv.at[c, x * hx + h], o_ss, o_rs, dev(z, y, co_, xo)
        )

    def attend(h):
        o_send[h] = jnp.dot(p_full[h], qkv_r[2, h], preferred_element_type=F32).astype(BF)
        loop(1, 2 * nx, lambda k: o_copy(h, k).start())

    loop(0, hx, attend)
    o_local = pltpu.make_async_copy(
        o_send.at[:, o_rows(x, c), :], m_recv.at[c, pl.ds(x * hx, hx)], o_ls
    )
    o_local.start()
    drain(o_send.at[:, pl.ds(0, (2 * nx - 1) * D.csites), :], o_ss, o_rs)
    o_local.wait()

    for n in range(3, 8):
        w_copies[n].wait()
    a_local.wait()
    a_copy.wait()

    half_rows = D.chains * D.csites
    for cc in range(2):
        for s in range(D.chains):
            mix[s * D.csites : (s + 1) * D.csites, :] = jnp.concatenate(
                [m_recv[cc, h, :, s * HEAD : (s + 1) * HEAD] for h in range(HEADS)], axis=-1
            )

        def mixing(cb, cc=cc):
            cols = pl.ds(pl.multiple_of(cb * 256, 256), 256)
            inc = jnp.dot(mix[...], w_buf[3, :, cols], preferred_element_type=F32)
            for s in range(D.chains):
                after = a_res[cc, s, :, cols].astype(F32) + inc[s * D.csites : (s + 1) * D.csites]
                for j in range(2):
                    c_f32[cb * 2 + j, pl.ds(cc * D.chains + s, D.csites, stride=D.pair), :] = after[
                        :, j * LANES : (j + 1) * LANES
                    ]

        loop(0, WIDTH // 256, mixing)

    def to_bf(dst):
        def part(i):
            rows = pl.ds(pl.multiple_of(i * 64, 64), 64)
            for j in range(SLABS):
                dst[rows, j * LANES : (j + 1) * LANES] = c_f32[j, rows, :].astype(BF)

        loop(0, D.rows // 64, part)

    def from_bf(src):
        def part(i):
            rows = pl.ds(pl.multiple_of(i * 64, 64), 64)
            for j in range(SLABS):
                c_f32[j, rows, :] = src[rows, j * LANES : (j + 1) * LANES].astype(F32)

        loop(0, D.rows // 64, part)

    def d_rows(i):
        return pl.ds(pl.multiple_of(i * D.drows, D.drows), D.drows)

    def exchange(src, dst, ss, rs, ls):
        def copy(k):
            p = lax.rem(d + k, nd)
            return remote(
                src.at[d_rows(p), :], dst.at[d_rows(d), :], ss, rs, dev(p // ny, lax.rem(p, ny), c, x)
            )

        keep = pltpu.make_async_copy(src.at[d_rows(d), :], dst.at[d_rows(d), :], ls)
        loop(1, nd, lambda k: copy(k).start())
        keep.start()
        drain(dst.at[pl.ds(0, (nd - 1) * D.drows), :], ss, rs)
        keep.wait()

    to_bf(c_send)
    exchange(c_send, c_recv, i_ss, i_rs, i_ls)
    from_bf(c_recv)

    col_scale = 1.0 / math.sqrt(HEAD)
    lane = lax.broadcasted_iota(jnp.int32, (1, 2 * HEAD), 1)

    def column(r):
        def rows_of(p):
            return pl.ds(pl.multiple_of(p * D.drows + r * D.pair, D.pair), D.pair)

        wide = jnp.concatenate(
            [
                jnp.concatenate([c_f32[j, rows_of(p), :] for p in range(nd)], axis=0)
                for j in range(SLABS)
            ],
            axis=1,
        )
        cn[...] = normed(wide, g2_ref[...])
        for m in range(3):
            c_qkv[m] = jnp.dot(cn[...], w_buf[4 + m], preferred_element_type=F32).astype(BF)

        def two_heads(p):
            cols = pl.ds(pl.multiple_of(p * 2 * HEAD, 2 * HEAD), 2 * HEAD)
            q, k, v = c_qkv[0, :, cols], c_qkv[1, :, cols], c_qkv[2, :, cols]
            mixed = None
            for side in range(2):
                mine = (lane < HEAD) if side == 0 else (lane >= HEAD)
                zero = jnp.zeros_like(k)
                scores = lax.dot_general(
                    q, jnp.where(mine, k, zero), NT, preferred_element_type=F32
                )
                prob = softmax(scores * col_scale)
                part = jnp.dot(prob, jnp.where(mine, v, zero), preferred_element_type=F32)
                mixed = part if mixed is None else mixed + part
            c_mix[:, cols] = mixed.astype(BF)

        loop(0, HEADS // 2, two_heads)
        change = jnp.dot(c_mix[...], w_buf[7], preferred_element_type=F32)
        for p in range(nd):
            rows = rows_of(p)
            for j in range(SLABS):
                c_f32[j, rows, :] += change[p * D.pair : (p + 1) * D.pair, j * LANES : (j + 1) * LANES]

    loop(0, D.cols, column)

    to_bf(r_send)
    exchange(r_send, r_recv, b_ss, b_rs, b_ls)
    from_bf(r_recv)

    def chain_rows(s):
        rows = pl.ds(s, D.csites, stride=D.pair)
        return jnp.concatenate([c_f32[j, rows, :] for j in range(SLABS)], axis=1).astype(BF)

    for s in range(D.chains):
        f_send[s] = chain_rows(other * D.chains + s)
    f_copy = remote(f_send, out_ref.at[:, a_half, :], f_sem.at[0], f_sem.at[1], sibling)
    f_copy.start()
    for s in range(D.chains):
        out_ref[s, a_half, :] = chain_rows(c * D.chains + s)
    f_copy.wait()


def on_device(D, a, g1, wq, wk, wv, wo, g2, cq, ck, cv, co):
    vmem = pl.BlockSpec(memory_space=pltpu.VMEM)
    hbm = pl.BlockSpec(memory_space=pl.ANY)
    sites = D.total_sites
    R = D.rows
    bf = lambda *shape: pltpu.VMEM(shape, BF)
    f32 = lambda *shape: pltpu.VMEM(shape, F32)
    sem = pltpu.SemaphoreType.DMA
    scratch = dict(
        w_buf=bf(8, WIDTH, WIDTH),
        xn=bf(R, WIDTH),
        qkv_s=bf(3, HEADS, D.sites, D.chains * HEAD),
        qkv_r=bf(3, D.hx, sites, D.chains * HEAD),
        l_own=f32(D.hx, D.half, sites),
        l_send=bf(D.hx, D.half, sites),
        l_recv=bf(D.hx, D.half, sites),
        y_send=bf(D.hx, D.half, sites),
        y_recv=bf(D.ny, D.hx, D.yrows, sites),
        z_sum=f32(D.hx, D.yrows, sites),
        z_send=bf(D.nz, D.zpad, sites),
        z_recv=bf(D.nz, D.zpad, sites),
        p_send=bf(D.zpad, sites),
        p_z=bf(D.nz, D.zpad, sites),
        p_full=bf(D.hx, sites, sites),
        o_send=bf(D.hx, sites, D.chains * HEAD),
        m_recv=bf(2, HEADS, D.csites, D.chains * HEAD),
        a_res=bf(2, D.chains, D.csites, WIDTH),
        mix=bf(D.chains * D.csites, WIDTH),
        c_f32=f32(SLABS, R, LANES),
        c_send=bf(R, WIDTH),
        c_recv=bf(R, WIDTH),
        cn=bf(D.col_len, WIDTH),
        c_qkv=bf(3, D.col_len, WIDTH),
        c_mix=bf(D.col_len, WIDTH),
        r_send=bf(R, WIDTH),
        r_recv=bf(R, WIDTH),
        f_send=bf(D.chains, D.csites, WIDTH),
        w_sem=sem((8,)),
        x_ss=sem((3,)), x_rs=sem((3,)), x_ls=sem((3,)), a_sem=sem((3,)),
        c_ss=sem((D.hx,)), c_rs=sem((D.hx,)), y_ss=sem((D.hx,)), y_rs=sem((D.hx,)),
        z_ss=sem, z_rs=sem, pz_ss=sem, pz_rs=sem, py_ss=sem, py_rs=sem, pc_sem=sem((2,)),
        o_ss=sem, o_rs=sem, o_ls=sem, i_ss=sem, i_rs=sem, i_ls=sem, b_ss=sem, b_rs=sem, b_ls=sem,
        f_sem=sem((2,)),
    )
    flops = 2 * (8 * R * WIDTH * WIDTH + 2 * D.hx * sites * sites * D.chains * HEAD)
    return pl.pallas_call(
        functools.partial(layer, D),
        out_shape=jax.ShapeDtypeStruct(a.shape, a.dtype),
        in_specs=[vmem] * 3 + [hbm] * 8,
        out_specs=vmem,
        scratch_shapes=list(scratch.values()),
        compiler_params=pltpu.CompilerParams(
            collective_id=0, has_side_effects=True, vmem_limit_bytes=60 * 2**20
        ),
        cost_estimate=pl.CostEstimate(flops=flops, bytes_accessed=12 * 2**20, transcendentals=2**21),
        name="msa_layer",
    )(a, g1.reshape(1, -1), g2.reshape(1, -1), wq, wk, wv, wo, cq, ck, cv, co)


def solution(mesh):
    nseq, nx = mesh.shape["seq"], mesh.shape["res"]
    ny = 4 if nseq >= 32 else 2

    def step(a, *rest):
        D = Dims(nseq, nx, ny, a.shape[0], a.shape[1])
        return on_device(D, a, *rest)

    in_specs = (P("seq", "res", None),) + (P(),) * 10
    return jax.shard_map(
        step, mesh=mesh, in_specs=in_specs, out_specs=P("seq", "res", None), check_vma=False
    )
```

```python
import functools
import math

import jax
import jax.numpy as jnp
from jax import lax
from jax.experimental import pallas as pl
from jax.experimental.pallas import tpu as pltpu
from jax.sharding import PartitionSpec as P

MESH = pl.DeviceIdType.MESH
HEADS = 12
HEAD = 64
WIDTH = HEADS * HEAD
LANES = 128
SLABS = WIDTH // LANES
BF = jnp.bfloat16
F32 = jnp.float32
NT = (((1,), (1,)), ((), ()))


class Dims:
    def __init__(self, nseq, nx, ny, chains, sites):
        self.nx, self.ny = nx, ny
        self.nz = nseq // (2 * ny)
        self.nd = self.ny * self.nz
        self.chains, self.sites = chains, sites
        self.rows = chains * sites
        self.hx = HEADS // nx
        self.total_sites = sites * nx
        self.parts = sites // (2 * self.nd)
        self.psites = sites // self.parts
        self.csites = self.psites // 2
        self.prows = self.psites * nx
        self.half = self.prows // 2
        self.yrows = self.half // ny
        self.zrows = self.yrows // self.nz
        self.zpad = -(-(self.hx * self.zrows) // 16) * 16
        self.pair = 2 * chains
        self.col_len = self.nd * self.pair
        self.total_seqs = nseq * chains
        assert self.csites == self.nd and self.pair == 8


def normed(wide, gain):
    center = wide - jnp.mean(wide, axis=-1, keepdims=True)
    spread = jnp.mean(center * center, axis=-1, keepdims=True)
    return (center * lax.rsqrt(spread + 1e-05) * gain).astype(BF)


def softmax(scores):
    top = jnp.max(scores, axis=-1, keepdims=True)
    e = jnp.exp(scores - top)
    return (e / jnp.sum(e, axis=-1, keepdims=True)).astype(BF)


def layer(
    D,
    a_ref, g1_ref, g2_ref,
    wq, wk, wv, wo, cq, ck, cv, co,
    out_ref,
    w_buf, xn, qkv_s, q_r, k_r, v_r, l_own, l_send, l_recv, y_send, y_recv, z_sum, z_send, z_recv,
    p_send, p_z, p_full, o_send, m_recv, a_res, mix, c_f32, c_send, c_recv, wide_buf, cn, c_qkv, c_mix,
    r_send, r_recv, f_send,
    w_sem, x_ss, x_rs, x_ls, a_ls, a_ss, a_rs, c_ss, c_rs, y_ss, y_rs, z_ss, z_rs, pz_ss, pz_rs, py_ss, py_rs,
    pc_ss, pc_rs, o_ss, o_rs, o_ls, i_ss, i_rs, i_ls, b_ss, b_rs, b_ls, f_ss, f_rs,
):
    nx, ny, nz, nd, hx = D.nx, D.ny, D.nz, D.nd, D.hx
    seq, x = lax.axis_index("seq"), lax.axis_index("res")
    c = lax.rem(seq, 2)
    d = seq // 2
    y = lax.rem(d, ny)
    z = d // ny
    other = 1 - c

    def dev(z_, y_, c_, x_):
        return ((z_ * ny + y_) * 2 + c_, x_)

    def dev_d(p):
        return dev(p // ny, lax.rem(p, ny), c, x)

    sibling = dev(z, y, other, x)

    def remote(src, dst, ss, rs, to):
        return pltpu.make_async_remote_copy(
            src_ref=src, dst_ref=dst, send_sem=ss, recv_sem=rs, device_id=to, device_id_type=MESH
        )

    def loop(lo, hi, body):
        def step(k, carry):
            body(k)
            return carry

        lax.fori_loop(lo, hi, step, 0)

    def drain(ref, *sems):
        for sem in sems:
            pltpu.make_async_copy(ref, ref, sem).wait()

    def block(i, n):
        return pl.ds(pl.multiple_of(i * n, n), n)

    weights = (wq, wk, wv, wo, cq, ck, cv, co)
    w_copies = [pltpu.make_async_copy(w, w_buf.at[n], w_sem.at[n]) for n, w in enumerate(weights)]
    for n in (1, 0, 2, 3, 4, 5, 6, 7):
        w_copies[n].start()

    bar = pltpu.get_barrier_semaphore()

    def greet(to):
        pl.semaphore_signal(bar, inc=1, device_id=to, device_id_type=MESH)

    def x_core(k):
        g = lax.rem(x * 2 + c + k, 2 * nx)
        return g // 2, lax.rem(g, 2)

    def greet_x(k):
        xo, co_ = x_core(k)
        greet(dev(z, y, co_, xo))

    loop(1, 2 * nx, greet_x)
    loop(1, nd, lambda k: greet(dev_d(lax.rem(d + k, nd))))

    def norm_rows(s):
        xn[block(s, D.sites), :] = normed(a_ref[s].astype(F32), g1_ref[...].reshape(1, WIDTH))

    loop(0, D.chains, norm_rows)

    def project(m):
        w_copies[m].wait()

        def columns(cb):
            cols = block(cb, 256)
            t = jnp.dot(xn[...], w_buf[m, :, cols], preferred_element_type=F32).astype(BF)
            for hh in range(4):
                qkv_s[m, cb * 4 + hh] = jnp.concatenate(
                    [
                        t[s * D.sites : (s + 1) * D.sites, hh * HEAD : (hh + 1) * HEAD]
                        for s in range(D.chains)
                    ],
                    axis=-1,
                )

        loop(0, WIDTH // 256, columns)

    my_sites = block(x, D.sites)
    my_part = block(x, D.psites)

    def kv_copies(m, dst, n):
        def copy(k):
            xo = lax.rem(x + k, nx)
            return remote(
                qkv_s.at[m, block(xo, hx)], dst.at[:, my_sites, :], x_ss.at[n], x_rs.at[n], dev(z, y, c, xo)
            )

        keep = pltpu.make_async_copy(qkv_s.at[m, block(x, hx)], dst.at[:, my_sites, :], x_ls.at[n])
        return copy, keep

    def q_copies(r):
        rows = pl.ds(r * D.psites, D.psites)

        def copy(k):
            xo = lax.rem(x + k, nx)
            return remote(
                qkv_s.at[0, block(xo, hx), rows, :],
                q_r.at[r, :, my_part, :],
                x_ss.at[2 + r],
                x_rs.at[2 + r],
                dev(z, y, c, xo),
            )

        keep = pltpu.make_async_copy(
            qkv_s.at[0, block(x, hx), rows, :], q_r.at[r, :, my_part, :], x_ls.at[2 + r]
        )
        return copy, keep

    def x_start(copies):
        copy, keep = copies
        loop(1, nx, lambda k: copy(k).start())
        keep.start()

    def x_wait(copies, ref, n):
        copies[1].wait()
        drain(ref, x_ss.at[n], x_rs.at[n])

    k_copies, v_copies = kv_copies(1, k_r, 0), kv_copies(2, v_r, 1)
    kv_size = pl.ds(0, (nx - 1) * D.sites)
    q_size = pl.ds(0, (nx - 1) * D.psites)

    project(1)
    pl.semaphore_wait(bar, nd - 1 + 2 * nx - 1)
    x_start(k_copies)
    project(0)
    for r in range(D.parts):
        x_start(q_copies(r))

    def a_rows(r, core):
        return block(r * 2 + core, D.csites)

    a_copies = []
    for r in range(D.parts):
        keep = pltpu.make_async_copy(a_ref.at[:, a_rows(r, c), :], a_res.at[r, c], a_ls.at[r])
        swap = remote(a_ref.at[:, a_rows(r, other), :], a_res.at[r, c], a_ss.at[r], a_rs.at[r], sibling)
        keep.start()
        swap.start()
        a_copies.append((keep, swap))

    project(2)

    scale = 1.0 / (math.sqrt(HEAD) * math.sqrt(D.total_seqs))
    own_half, far_half = block(c, D.half), block(other, D.half)

    def c_copy(r, h):
        return remote(l_send.at[r, h], l_recv.at[r, h], c_ss.at[r, h], c_rs.at[r, h], sibling)

    def logits(r):
        def far_part(h):
            far = lax.dot_general(q_r[r, h, far_half, :], k_r[h], NT, preferred_element_type=F32)
            l_send[r, h] = (far * scale).astype(BF)
            c_copy(r, h).start()

        def own_part(h):
            own = lax.dot_general(q_r[r, h, own_half, :], k_r[h], NT, preferred_element_type=F32)
            l_own[r, h] = own * scale

        loop(0, hx, far_part)
        loop(0, hx, own_part)

    def y_copy(r, k):
        yo = lax.rem(y + k, ny)
        return remote(
            y_send.at[r, :, block(yo, D.yrows), :], y_recv.at[r, y], y_ss.at[r], y_rs.at[r], dev(z, yo, c, x)
        )

    def core_sum(r):
        def one(h):
            c_copy(r, h).wait()
            total = l_own[r, h] + l_recv[r, h].astype(F32)
            l_own[r, h] = total
            y_send[r, h] = total.astype(BF)

        loop(0, hx, one)
        loop(1, ny, lambda k: y_copy(r, k).start())

    def z_copy(r, k):
        zo = lax.rem(z + k, nz)
        return remote(z_send.at[r, zo], z_recv.at[r, z], z_ss.at[r], z_rs.at[r], dev(zo, y, c, x))

    def y_sum(r):
        drain(y_recv.at[r, pl.ds(0, ny - 1)], y_ss.at[r], y_rs.at[r])
        for h in range(hx):
            total = l_own[r, h, block(y, D.yrows), :]
            for k in range(1, ny):
                total += y_recv[r, lax.rem(y + k, ny), h].astype(F32)
            z_sum[h] = total
        spare = D.zpad - hx * D.zrows
        for i in range(nz):
            part = [z_sum[h, i * D.zrows : (i + 1) * D.zrows, :] for h in range(hx)]
            if spare:
                part.append(jnp.zeros((spare, D.total_sites), F32))
            z_send[r, i] = jnp.concatenate(part, axis=0).astype(BF)
        loop(1, nz, lambda k: z_copy(r, k).start())

    def pz_copy(r, k):
        zo = lax.rem(z + k, nz)
        return remote(p_send.at[r], p_z.at[r, z], pz_ss.at[r], pz_rs.at[r], dev(zo, y, c, x))

    def z_softmax(r):
        drain(z_recv.at[r, pl.ds(0, nz - 1)], z_ss.at[r], z_rs.at[r])
        tied = z_send[r, z].astype(F32)
        for k in range(1, nz):
            tied += z_recv[r, lax.rem(z + k, nz)].astype(F32)
        prob = softmax(tied)
        p_send[r] = prob
        loop(1, nz, lambda k: pz_copy(r, k).start())
        p_z[r, z] = prob

    py_rows = block(c * ny + y, D.yrows)

    def py_copy(r, k):
        yo = lax.rem(y + k, ny)
        place = p_full.at[r, :, py_rows, :]
        return remote(place, place, py_ss.at[r], py_rs.at[r], dev(z, yo, c, x))

    def gather_z(r):
        drain(p_z.at[r, pl.ds(0, nz - 1)], pz_ss.at[r], pz_rs.at[r])
        for i in range(nz):
            wide = p_z[r, i].astype(F32)
            for h in range(hx):
                z_sum[h, i * D.zrows : (i + 1) * D.zrows, :] = wide[h * D.zrows : (h + 1) * D.zrows]
        p_full[r, :, py_rows, :] = z_sum[...].astype(BF)
        loop(1, ny, lambda k: py_copy(r, k).start())

    def pc_copy(r):
        place = p_full.at[r, :, own_half, :]
        return remote(place, place, pc_ss.at[r], pc_rs.at[r], sibling)

    def gather_y(r):
        drain(p_full.at[r, :, pl.ds(0, (ny - 1) * D.yrows), :], py_ss.at[r], py_rs.at[r])
        pc_copy(r).start()

    def o_rows(xo, core):
        return block(xo * 2 + core, D.csites)

    def o_copy(r, k):
        xo, co_ = x_core(k)
        return remote(
            o_send.at[r, :, o_rows(xo, co_), :],
            m_recv.at[r, c, block(x, hx)],
            o_ss.at[r],
            o_rs.at[r],
            dev(z, y, co_, xo),
        )

    def o_local(r):
        return pltpu.make_async_copy(
            o_send.at[r, :, o_rows(x, c), :], m_recv.at[r, c, block(x, hx)], o_ls.at[r]
        )

    def attend(r):
        pc_copy(r).wait()

        def one(h):
            o_send[r, h] = jnp.dot(p_full[r, h], v_r[h], preferred_element_type=F32).astype(BF)

        loop(0, hx, one)
        loop(1, 2 * nx, lambda k: o_copy(r, k).start())
        o_local(r).start()

    def pack(slabs):
        pieces = [v.reshape(nd, D.pair, LANES) for v in slabs]
        left = jnp.concatenate(pieces[: SLABS // 2], axis=-1)
        right = jnp.concatenate(pieces[SLABS // 2 :], axis=-1)
        return jnp.concatenate([left, right], axis=1).astype(BF).reshape(2 * D.col_len, WIDTH // 2)

    def unpack(packed):
        t = packed.reshape(nd, 2 * D.pair, WIDTH // 2).astype(F32)
        both = jnp.concatenate([t[:, : D.pair], t[:, D.pair :]], axis=-1)
        return both.reshape(D.col_len, WIDTH)

    def d_copies(r, src, dst, ss, rs, ls):
        def copy(k):
            p = lax.rem(d + k, nd)
            return remote(
                src.at[r, block(p, 2 * D.pair), :], dst.at[r, block(d, 2 * D.pair), :], ss.at[r], rs.at[r], dev_d(p)
            )

        mine = block(d, 2 * D.pair)
        keep = pltpu.make_async_copy(src.at[r, mine, :], dst.at[r, mine, :], ls.at[r])
        return copy, keep

    def d_start(r, *refs):
        copy, keep = d_copies(r, *refs)
        loop(1, nd, lambda k: copy(k).start())
        keep.start()

    def d_wait(r, src, dst, ss, rs, ls):
        d_copies(r, src, dst, ss, rs, ls)[1].wait()
        drain(dst.at[r, pl.ds(0, (nd - 1) * 2 * D.pair), :], ss.at[r], rs.at[r])

    into = (c_send, c_recv, i_ss, i_rs, i_ls)
    back = (r_send, r_recv, b_ss, b_rs, b_ls)

    def after_row(r):
        o_local(r).wait()
        drain(o_send.at[r, :, pl.ds(0, (2 * nx - 1) * D.csites), :], o_ss.at[r], o_rs.at[r])
        for copy in a_copies[r]:
            copy.wait()
        for cc in range(2):
            for s in range(D.chains):
                n = cc * D.chains + s
                mix[n * D.csites : (n + 1) * D.csites, :] = jnp.concatenate(
                    [m_recv[r, cc, h, :, s * HEAD : (s + 1) * HEAD] for h in range(HEADS)], axis=-1
                )

        def mixing(cb):
            cols = block(cb, 256)
            inc = jnp.dot(mix[...], w_buf[3, :, cols], preferred_element_type=F32)
            for cc in range(2):
                for s in range(D.chains):
                    n = cc * D.chains + s
                    after = a_res[r, cc, s, :, cols].astype(F32) + inc[n * D.csites : (n + 1) * D.csites]
                    for j in range(2):
                        c_f32[cb * 2 + j, pl.ds(n, D.csites, stride=D.pair), :] = after[
                            :, j * LANES : (j + 1) * LANES
                        ]

        loop(0, WIDTH // 256, mixing)
        c_send[r] = pack([c_f32[j] for j in range(SLABS)])
        d_start(r, *into)

    col_scale = 1.0 / math.sqrt(HEAD)
    lane = lax.broadcasted_iota(jnp.int32, (1, 2 * HEAD), 1)

    def column(r):
        d_wait(r, *into)
        wide = unpack(c_recv[r])
        wide_buf[...] = wide
        cn[...] = normed(wide, g2_ref[...].reshape(1, WIDTH))
        for m in range(3):
            c_qkv[m] = jnp.dot(cn[...], w_buf[4 + m], preferred_element_type=F32).astype(BF)

        def two_heads(p):
            cols = block(p, 2 * HEAD)
            q, k, v = c_qkv[0, :, cols], c_qkv[1, :, cols], c_qkv[2, :, cols]
            zero = jnp.zeros_like(k)
            mixed = None
            for side in range(2):
                mine = (lane < HEAD) if side == 0 else (lane >= HEAD)
                scores = lax.dot_general(
                    q, jnp.where(mine, k, zero), NT, preferred_element_type=F32
                )
                prob = softmax(scores * col_scale)
                part = jnp.dot(prob, jnp.where(mine, v, zero), preferred_element_type=F32)
                mixed = part if mixed is None else mixed + part
            c_mix[:, cols] = mixed.astype(BF)

        loop(0, HEADS // 2, two_heads)
        change = jnp.dot(c_mix[...], w_buf[7], preferred_element_type=F32)
        total = wide_buf[...] + change
        r_send[r] = pack([total[:, j * LANES : (j + 1) * LANES] for j in range(SLABS)])
        d_start(r, *back)

    def f_copy(r):
        return remote(f_send.at[r], out_ref.at[:, a_rows(r, c), :], f_ss.at[r], f_rs.at[r], sibling)

    def finish(r):
        d_wait(r, *back)
        total = unpack(r_recv[r])
        for j in range(SLABS):
            c_f32[j] = total[:, j * LANES : (j + 1) * LANES]

        def chain_rows(s):
            rows = pl.ds(s, D.csites, stride=D.pair)
            return jnp.concatenate([c_f32[j, rows, :] for j in range(SLABS)], axis=1).astype(BF)

        for s in range(D.chains):
            f_send[r, s] = chain_rows(other * D.chains + s)
        f_copy(r).start()
        for s in range(D.chains):
            out_ref[s, a_rows(r, c), :] = chain_rows(c * D.chains + s)

    q_sized = q_r.at[0, :, q_size, :]

    def first(r):
        x_wait(q_copies(r), q_sized, 2 + r)
        logits(r)

    x_wait(k_copies, k_r.at[:, kv_size, :], 0)
    first(0)
    x_start(v_copies)
    core_sum(0)
    first(1)
    y_sum(0)
    core_sum(1)
    z_softmax(0)
    y_sum(1)
    gather_z(0)
    z_softmax(1)
    gather_y(0)
    gather_z(1)
    x_wait(v_copies, v_r.at[:, kv_size, :], 1)
    attend(0)
    for n in range(3, 8):
        w_copies[n].wait()
    gather_y(1)
    after_row(0)
    attend(1)
    after_row(1)
    column(0)
    column(1)
    finish(0)
    finish(1)
    f_copy(0).wait()
    f_copy(1).wait()


def on_device(D, a, g1, wq, wk, wv, wo, g2, cq, ck, cv, co):
    vmem = pl.BlockSpec(memory_space=pltpu.VMEM)
    hbm = pl.BlockSpec(memory_space=pl.ANY)
    sites, N, L = D.total_sites, D.parts, D.chains * HEAD
    bf = lambda *shape: pltpu.VMEM(shape, BF)
    f32 = lambda *shape: pltpu.VMEM(shape, F32)
    sem = lambda *shape: pltpu.SemaphoreType.DMA(shape)
    scratch = dict(
        w_buf=bf(8, WIDTH, WIDTH),
        xn=bf(D.rows, WIDTH),
        qkv_s=bf(3, HEADS, D.sites, L),
        q_r=bf(N, D.hx, D.prows, L),
        k_r=bf(D.hx, sites, L),
        v_r=bf(D.hx, sites, L),
        l_own=f32(N, D.hx, D.half, sites),
        l_send=bf(N, D.hx, D.half, sites),
        l_recv=bf(N, D.hx, D.half, sites),
        y_send=bf(N, D.hx, D.half, sites),
        y_recv=bf(N, D.ny, D.hx, D.yrows, sites),
        z_sum=f32(D.hx, D.yrows, sites),
        z_send=bf(N, D.nz, D.zpad, sites),
        z_recv=bf(N, D.nz, D.zpad, sites),
        p_send=bf(N, D.zpad, sites),
        p_z=bf(N, D.nz, D.zpad, sites),
        p_full=bf(N, D.hx, D.prows, sites),
        o_send=bf(N, D.hx, D.prows, L),
        m_recv=bf(N, 2, HEADS, D.csites, L),
        a_res=bf(N, 2, D.chains, D.csites, WIDTH),
        mix=bf(D.pair * D.csites, WIDTH),
        c_f32=f32(SLABS, D.col_len, LANES),
        c_send=bf(N, 2 * D.col_len, WIDTH // 2),
        c_recv=bf(N, 2 * D.col_len, WIDTH // 2),
        wide_buf=f32(D.col_len, WIDTH),
        cn=bf(D.col_len, WIDTH),
        c_qkv=bf(3, D.col_len, WIDTH),
        c_mix=bf(D.col_len, WIDTH),
        r_send=bf(N, 2 * D.col_len, WIDTH // 2),
        r_recv=bf(N, 2 * D.col_len, WIDTH // 2),
        f_send=bf(N, D.chains, D.csites, WIDTH),
        w_sem=sem(8),
        x_ss=sem(2 + N), x_rs=sem(2 + N), x_ls=sem(2 + N),
        a_ls=sem(N), a_ss=sem(N), a_rs=sem(N),
        c_ss=sem(N, D.hx), c_rs=sem(N, D.hx),
        y_ss=sem(N), y_rs=sem(N), z_ss=sem(N), z_rs=sem(N),
        pz_ss=sem(N), pz_rs=sem(N), py_ss=sem(N), py_rs=sem(N), pc_ss=sem(N), pc_rs=sem(N),
        o_ss=sem(N), o_rs=sem(N), o_ls=sem(N),
        i_ss=sem(N), i_rs=sem(N), i_ls=sem(N), b_ss=sem(N), b_rs=sem(N), b_ls=sem(N),
        f_ss=sem(N), f_rs=sem(N),
    )
    flops = 2 * (8 * D.rows * WIDTH * WIDTH + 2 * D.hx * sites * sites * L)
    return pl.pallas_call(
        functools.partial(layer, D),
        out_shape=jax.ShapeDtypeStruct(a.shape, a.dtype),
        in_specs=[vmem] * 3 + [hbm] * 8,
        out_specs=vmem,
        scratch_shapes=list(scratch.values()),
        compiler_params=pltpu.CompilerParams(
            collective_id=0, has_side_effects=True, vmem_limit_bytes=60 * 2**20
        ),
        cost_estimate=pl.CostEstimate(flops=flops, bytes_accessed=12 * 2**20, transcendentals=2**21),
        name="msa_layer",
    )(a, g1, g2, wq, wk, wv, wo, cq, ck, cv, co)


def solution(mesh):
    nseq, nx = mesh.shape["seq"], mesh.shape["res"]
    ny = 4

    def step(a, *rest):
        D = Dims(nseq, nx, ny, a.shape[0], a.shape[1])
        return on_device(D, a, *rest)

    in_specs = (P("seq", "res", None),) + (P(),) * 10
    return jax.shard_map(
        step, mesh=mesh, in_specs=in_specs, out_specs=P("seq", "res", None), check_vma=False
    )
```

```python
import functools
import math

import jax
import jax.numpy as jnp
from jax import lax
from jax.experimental import pallas as pl
from jax.experimental.pallas import tpu as pltpu
from jax.sharding import PartitionSpec as P

MESH = pl.DeviceIdType.MESH
HEADS = 12
HEAD = 64
WIDTH = HEADS * HEAD
LANES = 128
SLABS = WIDTH // LANES
BF = jnp.bfloat16
F32 = jnp.float32
NT = (((1,), (1,)), ((), ()))


class Dims:
    def __init__(self, nseq, nx, ny, chains, sites):
        self.nx, self.ny = nx, ny
        self.nz = nseq // (2 * ny)
        self.nd = self.ny * self.nz
        self.chains, self.sites = chains, sites
        self.rows = chains * sites
        self.hx = HEADS // nx
        self.total_sites = sites * nx
        self.parts = sites // (2 * self.nd)
        self.psites = sites // self.parts
        self.csites = self.psites // 2
        self.prows = self.psites * nx
        self.half = self.prows // 2
        self.yrows = self.half // ny
        self.zrows = self.yrows // self.nz
        self.pair = 2 * chains
        self.col_len = self.nd * self.pair
        self.total_seqs = nseq * chains
        assert self.csites == self.nd and self.pair == 8 and self.zrows == 4


def normed(wide, gain):
    center = wide - jnp.mean(wide, axis=-1, keepdims=True)
    spread = jnp.mean(center * center, axis=-1, keepdims=True)
    return (center * lax.rsqrt(spread + 1e-05) * gain).astype(BF)


def softmax(scores):
    top = jnp.max(scores, axis=-1, keepdims=True)
    e = jnp.exp(scores - top)
    return e / jnp.sum(e, axis=-1, keepdims=True)


def layer(
    D,
    a_ref, g1_ref, g2_ref,
    wq, wk, wv, wo, cq, ck, cv, co,
    out_ref,
    w_buf, xn, qkv_s, kv_r, q_r, l_own, l_send, l_recv, y_send, y_recv, z_send, z_recv,
    p_send, p_z, p_full, o_send, m_recv, a_res, mix, c_f32, c_send, c_recv, wide_buf, cn, c_qkv, c_mix,
    r_send, r_recv, f_send,
    w_sem, x_ss, x_rs, x_ls, a_ls, a_ss, a_rs, c_ss, c_rs, y_ss, y_rs, z_ss, z_rs, pz_ss, pz_rs, py_ss, py_rs,
    pc_ss, pc_rs, o_ss, o_rs, o_ls, i_ss, i_rs, i_ls, b_ss, b_rs, b_ls, f_ss, f_rs,
):
    nx, ny, nz, nd, hx = D.nx, D.ny, D.nz, D.nd, D.hx
    seq, x = lax.axis_index("seq"), lax.axis_index("res")
    c = lax.rem(seq, 2)
    d = seq // 2
    y = lax.rem(d, ny)
    z = d // ny
    other = 1 - c

    def dev(z_, y_, c_, x_):
        return ((z_ * ny + y_) * 2 + c_, x_)

    def dev_d(p):
        return dev(p // ny, lax.rem(p, ny), c, x)

    sibling = dev(z, y, other, x)

    def remote(src, dst, ss, rs, to):
        return pltpu.make_async_remote_copy(
            src_ref=src, dst_ref=dst, send_sem=ss, recv_sem=rs, device_id=to, device_id_type=MESH
        )

    def loop(lo, hi, body):
        def step(k, carry):
            body(k)
            return carry

        lax.fori_loop(lo, hi, step, 0)

    def drain(ref, *sems):
        for sem in sems:
            pltpu.make_async_copy(ref, ref, sem).wait()

    def block(i, n):
        return pl.ds(pl.multiple_of(i * n, n), n)

    weights = (wk, wv, wq, wo, cq, ck, cv, co)
    w_copies = [pltpu.make_async_copy(w, w_buf.at[n], w_sem.at[n]) for n, w in enumerate(weights)]
    for n in (0, 2):
        w_copies[n].start()

    bar = pltpu.get_barrier_semaphore()

    def greet(to):
        pl.semaphore_signal(bar, inc=1, device_id=to, device_id_type=MESH)

    def x_core(k):
        g = lax.rem(x * 2 + c + k, 2 * nx)
        return g // 2, lax.rem(g, 2)

    def greet_x(k):
        xo, co_ = x_core(k)
        greet(dev(z, y, co_, xo))

    loop(1, 2 * nx, greet_x)
    loop(1, nd, lambda k: greet(dev_d(lax.rem(d + k, nd))))

    def norm_rows(s):
        xn[block(s, D.sites), :] = normed(a_ref[s].astype(F32), g1_ref[...].reshape(1, WIDTH))

    loop(0, D.chains, norm_rows)

    def project(m, h):
        w = jnp.concatenate(
            [w_buf[m, :, (g * hx + h) * HEAD : (g * hx + h + 1) * HEAD] for g in range(nx)], axis=-1
        )
        t = jnp.dot(xn[...], w, preferred_element_type=F32).astype(BF)
        for g in range(nx):
            qkv_s[m, h, g] = jnp.concatenate(
                [
                    t[s * D.sites : (s + 1) * D.sites, g * HEAD : (g + 1) * HEAD]
                    for s in range(D.chains)
                ],
                axis=-1,
            )

    my_sites = block(x, D.sites)
    my_part = block(x, D.psites)

    class Cross:
        def __init__(self, m, h, r=None):
            self.sem = m * hx + h if r is None else (2 + r) * hx + h
            if r is None:
                self.dst = kv_r.at[m, h, my_sites, :]
                self.size = kv_r.at[m, h, pl.ds(0, (nx - 1) * D.sites), :]
                self.src = lambda g: qkv_s.at[m, h, g]
            else:
                self.dst = q_r.at[r, h, my_part, :]
                self.size = q_r.at[r, h, pl.ds(0, (nx - 1) * D.psites), :]
                self.src = lambda g: qkv_s.at[2, h, g, pl.ds(r * D.psites, D.psites), :]

        def copy(self, k):
            xo = lax.rem(x + k, nx)
            return remote(
                self.src(xo), self.dst, x_ss.at[self.sem], x_rs.at[self.sem], dev(z, y, c, xo)
            )

        def keep(self):
            return pltpu.make_async_copy(self.src(x), self.dst, x_ls.at[self.sem])

        def start(self):
            loop(1, nx, lambda k: self.copy(k).start())
            self.keep().start()

        def wait(self):
            self.keep().wait()
            drain(self.size, x_ss.at[self.sem], x_rs.at[self.sem])

    scale = 1.0 / (math.sqrt(HEAD) * math.sqrt(D.total_seqs))
    own_half, far_half = block(c, D.half), block(other, D.half)

    def c_copy(r, h):
        return remote(l_send.at[r, h], l_recv.at[r, h], c_ss.at[r, h], c_rs.at[r, h], sibling)

    def logits(r, h):
        if r == 0:
            Cross(0, h).wait()
        Cross(2, h, r).wait()
        far = lax.dot_general(q_r[r, h, far_half, :], kv_r[0, h], NT, preferred_element_type=F32)
        l_send[r, h] = (far * scale).astype(BF)
        c_copy(r, h).start()
        own = lax.dot_general(q_r[r, h, own_half, :], kv_r[0, h], NT, preferred_element_type=F32)
        l_own[r, h] = own * scale

    def y_copy(r, h, k):
        yo = lax.rem(y + k, ny)
        return remote(
            y_send.at[r, h, block(yo, D.yrows), :],
            y_recv.at[r, h, y],
            y_ss.at[r, h],
            y_rs.at[r, h],
            dev(z, yo, c, x),
        )

    def core_sum(r, h):
        c_copy(r, h).wait()
        total = l_own[r, h] + l_recv[r, h].astype(F32)
        l_own[r, h] = total
        y_send[r, h] = total.astype(BF)
        loop(1, ny, lambda k: y_copy(r, h, k).start())

    zr, slabs = D.zrows, D.total_sites // LANES
    zt = zr * slabs

    def fold(rows):
        n = rows.shape[0] // zr
        return jnp.concatenate(
            [
                rows[i * zr : (i + 1) * zr, j * LANES : (j + 1) * LANES]
                for i in range(n)
                for j in range(slabs)
            ],
            axis=0,
        )

    def unfold(tiles):
        n = tiles.shape[0] // zt
        return jnp.concatenate(
            [
                jnp.concatenate(
                    [tiles[i * zt + j * zr : i * zt + (j + 1) * zr] for i in range(n)], axis=0
                )
                for j in range(slabs)
            ],
            axis=1,
        )

    z_size = pl.ds(0, (nz - 1) * zt)

    def z_copy(r, h, k):
        zo = lax.rem(z + k, nz)
        return remote(
            z_send.at[r, h, block(zo, zt), :],
            z_recv.at[r, h, block(z, zt), :],
            z_ss.at[r, h],
            z_rs.at[r, h],
            dev(zo, y, c, x),
        )

    def y_sum(r, h):
        drain(y_recv.at[r, h, pl.ds(0, ny - 1)], y_ss.at[r, h], y_rs.at[r, h])
        total = l_own[r, h, block(y, D.yrows), :]
        for k in range(1, ny):
            total += y_recv[r, h, lax.rem(y + k, ny)].astype(F32)
        z_send[r, h] = fold(total).astype(BF)
        loop(1, nz, lambda k: z_copy(r, h, k).start())

    def pz_copy(r, h, k):
        zo = lax.rem(z + k, nz)
        return remote(
            p_send.at[r, h], p_z.at[r, h, block(z, zt), :], pz_ss.at[r, h], pz_rs.at[r, h], dev(zo, y, c, x)
        )

    def z_softmax(r, h):
        drain(z_recv.at[r, h, z_size, :], z_ss.at[r, h], z_rs.at[r, h])
        tied = z_send[r, h, block(z, zt), :].astype(F32)
        for k in range(1, nz):
            tied += z_recv[r, h, block(lax.rem(z + k, nz), zt), :].astype(F32)
        prob = fold(softmax(unfold(tied))).astype(BF)
        p_send[r, h] = prob
        loop(1, nz, lambda k: pz_copy(r, h, k).start())
        p_z[r, h, block(z, zt), :] = prob

    py_rows = block(c * ny + y, D.yrows)

    def py_copy(r, h, k):
        yo = lax.rem(y + k, ny)
        place = p_full.at[r, h, py_rows, :]
        return remote(place, place, py_ss.at[r, h], py_rs.at[r, h], dev(z, yo, c, x))

    def gather_z(r, h):
        drain(p_z.at[r, h, z_size, :], pz_ss.at[r, h], pz_rs.at[r, h])
        p_full[r, h, py_rows, :] = unfold(p_z[r, h].astype(F32)).astype(BF)
        loop(1, ny, lambda k: py_copy(r, h, k).start())

    def pc_copy(r, h):
        place = p_full.at[r, h, own_half, :]
        return remote(place, place, pc_ss.at[r, h], pc_rs.at[r, h], sibling)

    def gather_y(r, h):
        drain(p_full.at[r, h, pl.ds(0, (ny - 1) * D.yrows), :], py_ss.at[r, h], py_rs.at[r, h])
        pc_copy(r, h).start()

    def o_rows(xo, core):
        return block(xo * 2 + core, D.csites)

    def o_copy(r, h, k):
        xo, co_ = x_core(k)
        return remote(
            o_send.at[r, h, o_rows(xo, co_), :],
            m_recv.at[r, c, x * hx + h],
            o_ss.at[r, h],
            o_rs.at[r, h],
            dev(z, y, co_, xo),
        )

    def o_local(r, h):
        return pltpu.make_async_copy(
            o_send.at[r, h, o_rows(x, c), :], m_recv.at[r, c, x * hx + h], o_ls.at[r, h]
        )

    def attend(r, h):
        if r == 0:
            Cross(1, h).wait()
        pc_copy(r, h).wait()
        o_send[r, h] = jnp.dot(p_full[r, h], kv_r[1, h], preferred_element_type=F32).astype(BF)
        loop(1, 2 * nx, lambda k: o_copy(r, h, k).start())
        o_local(r, h).start()

    def pack(slabs):
        pieces = [v.reshape(nd, D.pair, LANES) for v in slabs]
        left = jnp.concatenate(pieces[: SLABS // 2], axis=-1)
        right = jnp.concatenate(pieces[SLABS // 2 :], axis=-1)
        return jnp.concatenate([left, right], axis=1).astype(BF).reshape(2 * D.col_len, WIDTH // 2)

    def unpack(packed):
        t = packed.reshape(nd, 2 * D.pair, WIDTH // 2).astype(F32)
        both = jnp.concatenate([t[:, : D.pair], t[:, D.pair :]], axis=-1)
        return both.reshape(D.col_len, WIDTH)

    def d_copies(r, src, dst, ss, rs, ls):
        def copy(k):
            p = lax.rem(d + k, nd)
            return remote(
                src.at[r, block(p, 2 * D.pair), :], dst.at[r, block(d, 2 * D.pair), :], ss.at[r], rs.at[r], dev_d(p)
            )

        mine = block(d, 2 * D.pair)
        keep = pltpu.make_async_copy(src.at[r, mine, :], dst.at[r, mine, :], ls.at[r])
        return copy, keep

    def d_start(r, *refs):
        copy, keep = d_copies(r, *refs)
        loop(1, nd, lambda k: copy(k).start())
        keep.start()

    def d_wait(r, src, dst, ss, rs, ls):
        d_copies(r, src, dst, ss, rs, ls)[1].wait()
        drain(dst.at[r, pl.ds(0, (nd - 1) * 2 * D.pair), :], ss.at[r], rs.at[r])

    into = (c_send, c_recv, i_ss, i_rs, i_ls)
    back = (r_send, r_recv, b_ss, b_rs, b_ls)

    def a_rows(r, core):
        return block(r * 2 + core, D.csites)

    def residual_copies():
        copies = []
        for r in range(D.parts):
            keep = pltpu.make_async_copy(a_ref.at[:, a_rows(r, c), :], a_res.at[r, c], a_ls.at[r])
            swap = remote(a_ref.at[:, a_rows(r, other), :], a_res.at[r, c], a_ss.at[r], a_rs.at[r], sibling)
            keep.start()
            swap.start()
            copies.append((keep, swap))
        return copies

    def after_row(r):
        for h in range(hx):
            o_local(r, h).wait()
            drain(o_send.at[r, h, pl.ds(0, (2 * nx - 1) * D.csites), :], o_ss.at[r, h], o_rs.at[r, h])
        for copy in a_copies[r]:
            copy.wait()
        for cc in range(2):
            for s in range(D.chains):
                n = cc * D.chains + s
                mix[n * D.csites : (n + 1) * D.csites, :] = jnp.concatenate(
                    [m_recv[r, cc, h, :, s * HEAD : (s + 1) * HEAD] for h in range(HEADS)], axis=-1
                )

        def mixing(cb):
            cols = block(cb, 256)
            inc = jnp.dot(mix[...], w_buf[3, :, cols], preferred_element_type=F32)
            for cc in range(2):
                for s in range(D.chains):
                    n = cc * D.chains + s
                    after = a_res[r, cc, s, :, cols].astype(F32) + inc[n * D.csites : (n + 1) * D.csites]
                    for j in range(2):
                        c_f32[cb * 2 + j, pl.ds(n, D.csites, stride=D.pair), :] = after[
                            :, j * LANES : (j + 1) * LANES
                        ]

        loop(0, WIDTH // 256, mixing)
        c_send[r] = pack([c_f32[j] for j in range(SLABS)])
        d_start(r, *into)

    col_scale = 1.0 / math.sqrt(HEAD)
    lane = lax.broadcasted_iota(jnp.int32, (1, 2 * HEAD), 1)

    def column(r):
        d_wait(r, *into)
        wide = unpack(c_recv[r])
        wide_buf[...] = wide
        cn[...] = normed(wide, g2_ref[...].reshape(1, WIDTH))
        for m in range(3):
            c_qkv[m] = jnp.dot(cn[...], w_buf[4 + m], preferred_element_type=F32).astype(BF)

        def two_heads(p):
            cols = block(p, 2 * HEAD)
            q, k, v = c_qkv[0, :, cols], c_qkv[1, :, cols], c_qkv[2, :, cols]
            zero = jnp.zeros_like(k)
            mixed = None
            for side in range(2):
                mine = (lane < HEAD) if side == 0 else (lane >= HEAD)
                scores = lax.dot_general(
                    q, jnp.where(mine, k, zero), NT, preferred_element_type=F32
                )
                prob = softmax(scores * col_scale).astype(BF)
                part = jnp.dot(prob, jnp.where(mine, v, zero), preferred_element_type=F32)
                mixed = part if mixed is None else mixed + part
            c_mix[:, cols] = mixed.astype(BF)

        loop(0, HEADS // 2, two_heads)
        change = jnp.dot(c_mix[...], w_buf[7], preferred_element_type=F32)
        total = wide_buf[...] + change
        r_send[r] = pack([total[:, j * LANES : (j + 1) * LANES] for j in range(SLABS)])
        d_start(r, *back)

    def f_copy(r):
        return remote(f_send.at[r], out_ref.at[:, a_rows(r, c), :], f_ss.at[r], f_rs.at[r], sibling)

    def finish(r):
        d_wait(r, *back)
        total = unpack(r_recv[r])
        for j in range(SLABS):
            c_f32[j] = total[:, j * LANES : (j + 1) * LANES]

        def chain_rows(s):
            rows = pl.ds(s, D.csites, stride=D.pair)
            return jnp.concatenate([c_f32[j, rows, :] for j in range(SLABS)], axis=1).astype(BF)

        for s in range(D.chains):
            f_send[r, s] = chain_rows(other * D.chains + s)
        f_copy(r).start()
        for s in range(D.chains):
            out_ref[s, a_rows(r, c), :] = chain_rows(c * D.chains + s)

    for m in (0, 2):
        w_copies[m].wait()
    for n in (1, 3, 4, 5, 6, 7):
        w_copies[n].start()

    def first(h):
        Cross(0, h).start()
        Cross(2, h, 0).start()

    project(0, 0)
    project(2, 0)
    pl.semaphore_wait(bar, nd - 1 + 2 * nx - 1)
    first(0)
    project(0, 1)
    project(2, 1)
    first(1)
    project(0, 2)
    project(2, 2)
    a_copies = residual_copies()
    w_copies[1].wait()
    for h in range(hx):
        project(1, h)

    def queries(h):
        Cross(2, h, 1).start()

    def values(h):
        Cross(1, h).start()

    def weights_in():
        for n in range(3, 8):
            w_copies[n].wait()

    plan = (
        (logits, 0, 0), (first, 2), (core_sum, 0, 0), (logits, 0, 1), (queries, 0), (queries, 1), (queries, 2),
        (core_sum, 0, 1), (y_sum, 0, 0), (logits, 0, 2), (values, 0), (values, 1), (values, 2),
        (core_sum, 0, 2), (y_sum, 0, 1), (z_softmax, 0, 0), (logits, 1, 0), (core_sum, 1, 0), (y_sum, 0, 2),
        (z_softmax, 0, 1), (gather_z, 0, 0), (logits, 1, 1), (core_sum, 1, 1), (y_sum, 1, 0), (z_softmax, 0, 2),
        (gather_z, 0, 1), (gather_y, 0, 0), (logits, 1, 2), (core_sum, 1, 2), (y_sum, 1, 1), (attend, 0, 0),
        (z_softmax, 1, 0), (gather_z, 0, 2), (gather_y, 0, 1), (y_sum, 1, 2), (attend, 0, 1), (z_softmax, 1, 1),
        (gather_z, 1, 0), (gather_y, 0, 2), (weights_in,), (attend, 0, 2), (z_softmax, 1, 2), (gather_z, 1, 1),
        (gather_y, 1, 0), (attend, 1, 0), (gather_z, 1, 2), (after_row, 0), (gather_y, 1, 1), (attend, 1, 1),
        (gather_y, 1, 2), (attend, 1, 2), (after_row, 1), (column, 0), (column, 1), (finish, 0), (finish, 1),
    )
    for step, *args in plan:
        step(*args)
    f_copy(0).wait()
    f_copy(1).wait()


def on_device(D, a, g1, wq, wk, wv, wo, g2, cq, ck, cv, co):
    vmem = pl.BlockSpec(memory_space=pltpu.VMEM)
    hbm = pl.BlockSpec(memory_space=pl.ANY)
    sites, N, H, L = D.total_sites, D.parts, D.hx, D.chains * HEAD
    bf = lambda *shape: pltpu.VMEM(shape, BF)
    f32 = lambda *shape: pltpu.VMEM(shape, F32)
    sem = lambda *shape: pltpu.SemaphoreType.DMA(shape)
    scratch = dict(
        w_buf=bf(8, WIDTH, WIDTH),
        xn=bf(D.rows, WIDTH),
        qkv_s=bf(3, D.hx, D.nx, D.sites, L),
        kv_r=bf(2, H, sites, L),
        q_r=bf(N, H, D.prows, L),
        l_own=f32(N, H, D.half, sites),
        l_send=bf(N, H, D.half, sites),
        l_recv=bf(N, H, D.half, sites),
        y_send=bf(N, H, D.half, sites),
        y_recv=bf(N, H, D.ny, D.yrows, sites),
        z_send=bf(N, H, D.yrows * sites // LANES, LANES),
        z_recv=bf(N, H, D.yrows * sites // LANES, LANES),
        p_send=bf(N, H, D.zrows * sites // LANES, LANES),
        p_z=bf(N, H, D.yrows * sites // LANES, LANES),
        p_full=bf(N, H, D.prows, sites),
        o_send=bf(N, H, D.prows, L),
        m_recv=bf(N, 2, HEADS, D.csites, L),
        a_res=bf(N, 2, D.chains, D.csites, WIDTH),
        mix=bf(D.pair * D.csites, WIDTH),
        c_f32=f32(SLABS, D.col_len, LANES),
        c_send=bf(N, 2 * D.col_len, WIDTH // 2),
        c_recv=bf(N, 2 * D.col_len, WIDTH // 2),
        wide_buf=f32(D.col_len, WIDTH),
        cn=bf(D.col_len, WIDTH),
        c_qkv=bf(3, D.col_len, WIDTH),
        c_mix=bf(D.col_len, WIDTH),
        r_send=bf(N, 2 * D.col_len, WIDTH // 2),
        r_recv=bf(N, 2 * D.col_len, WIDTH // 2),
        f_send=bf(N, D.chains, D.csites, WIDTH),
        w_sem=sem(8),
        x_ss=sem((2 + N) * H), x_rs=sem((2 + N) * H), x_ls=sem((2 + N) * H),
        a_ls=sem(N), a_ss=sem(N), a_rs=sem(N),
        c_ss=sem(N, H), c_rs=sem(N, H), y_ss=sem(N, H), y_rs=sem(N, H), z_ss=sem(N, H), z_rs=sem(N, H),
        pz_ss=sem(N, H), pz_rs=sem(N, H), py_ss=sem(N, H), py_rs=sem(N, H), pc_ss=sem(N, H), pc_rs=sem(N, H),
        o_ss=sem(N, H), o_rs=sem(N, H), o_ls=sem(N, H),
        i_ss=sem(N), i_rs=sem(N), i_ls=sem(N), b_ss=sem(N), b_rs=sem(N), b_ls=sem(N),
        f_ss=sem(N), f_rs=sem(N),
    )
    flops = 2 * (8 * D.rows * WIDTH * WIDTH + 2 * D.hx * sites * sites * L)
    return pl.pallas_call(
        functools.partial(layer, D),
        out_shape=jax.ShapeDtypeStruct(a.shape, a.dtype),
        in_specs=[vmem] * 3 + [hbm] * 8,
        out_specs=vmem,
        scratch_shapes=list(scratch.values()),
        compiler_params=pltpu.CompilerParams(
            collective_id=0, has_side_effects=True, vmem_limit_bytes=60 * 2**20
        ),
        cost_estimate=pl.CostEstimate(flops=flops, bytes_accessed=12 * 2**20, transcendentals=2**21),
        name="msa_layer",
    )(a, g1, g2, wq, wk, wv, wo, cq, ck, cv, co)


def solution(mesh):
    nseq, nx = mesh.shape["seq"], mesh.shape["res"]
    ny = 4

    def step(a, *rest):
        D = Dims(nseq, nx, ny, a.shape[0], a.shape[1])
        return on_device(D, a, *rest)

    in_specs = (P("seq", "res", None),) + (P(),) * 10
    return jax.shard_map(
        step, mesh=mesh, in_specs=in_specs, out_specs=P("seq", "res", None), check_vma=False
    )
```

```python
import functools
import math

import jax
import jax.numpy as jnp
from jax import lax
from jax.experimental import pallas as pl
from jax.experimental.pallas import tpu as pltpu
from jax.sharding import PartitionSpec as P

MESH = pl.DeviceIdType.MESH
HEADS = 12
HEAD = 64
WIDTH = HEADS * HEAD
LANES = 128
SLABS = WIDTH // LANES
BF = jnp.bfloat16
F32 = jnp.float32
NT = (((1,), (1,)), ((), ()))


class Dims:
    def __init__(self, nseq, nx, ny, chains, sites):
        self.nx, self.ny = nx, ny
        self.nz = nseq // (2 * ny)
        self.nd = self.ny * self.nz
        self.chains, self.sites = chains, sites
        self.rows = chains * sites
        self.hx = HEADS // nx
        self.total_sites = sites * nx
        self.parts = sites // (2 * self.nd)
        self.psites = sites // self.parts
        self.csites = self.psites // 2
        self.prows = self.psites * nx
        self.half = self.prows // 2
        self.yrows = self.half // ny
        self.zrows = self.yrows // self.nz
        self.pair = 2 * chains
        self.col_len = self.nd * self.pair
        self.total_seqs = nseq * chains
        assert self.csites == self.nd and self.pair == 8 and self.zrows == 4


def normed(wide, gain):
    center = wide - jnp.mean(wide, axis=-1, keepdims=True)
    spread = jnp.mean(center * center, axis=-1, keepdims=True)
    return (center * lax.rsqrt(spread + 1e-05) * gain).astype(BF)


def softmax(scores):
    top = jnp.max(scores, axis=-1, keepdims=True)
    e = jnp.exp(scores - top)
    return e / jnp.sum(e, axis=-1, keepdims=True)


def layer(
    D,
    a_ref, g1_ref, g2_ref,
    wq, wk, wv, wo, cq, ck, cv, co,
    out_ref,
    w_buf, xn, qkv_s, kv_r, q_r, l_own, l_send, l_recv, y_send, y_recv, z_send, z_recv,
    p_send, p_z, p_full, o_send, m_recv, a_res, mix, c_f32, c_send, c_recv, wide_buf, cn, c_qkv, c_mix,
    r_send, r_recv, f_send,
    w_sem, x_ss, x_rs, x_ls, a_ls, a_ss, a_rs, c_ss, c_rs, y_ss, y_rs, z_ss, z_rs, pz_ss, pz_rs, py_ss, py_rs,
    pc_ss, pc_rs, o_ss, o_rs, o_ls, i_ss, i_rs, i_ls, b_ss, b_rs, b_ls, f_ss, f_rs,
):
    nx, ny, nz, nd, hx = D.nx, D.ny, D.nz, D.nd, D.hx
    seq, x = lax.axis_index("seq"), lax.axis_index("res")
    c = lax.rem(seq, 2)
    d = seq // 2
    y = lax.rem(d, ny)
    z = d // ny
    other = 1 - c

    def dev(z_, y_, c_, x_):
        return ((z_ * ny + y_) * 2 + c_, x_)

    def dev_d(p):
        return dev(p // ny, lax.rem(p, ny), c, x)

    sibling = dev(z, y, other, x)

    def remote(src, dst, ss, rs, to):
        return pltpu.make_async_remote_copy(
            src_ref=src, dst_ref=dst, send_sem=ss, recv_sem=rs, device_id=to, device_id_type=MESH
        )

    def loop(lo, hi, body):
        def step(k, carry):
            body(k)
            return carry

        lax.fori_loop(lo, hi, step, 0)

    def drain(ref, *sems):
        for sem in sems:
            pltpu.make_async_copy(ref, ref, sem).wait()

    def block(i, n):
        return pl.ds(pl.multiple_of(i * n, n), n)

    def turn(i, n):
        j = n - 1 - i
        far = (j + 1) // 2
        return lax.rem(far + (n - 2 * far) * lax.rem(j + 1, 2), n)

    weights = (wk, wv, wq, wo, cq, ck, cv, co)
    w_copies = [pltpu.make_async_copy(w, w_buf.at[n], w_sem.at[n]) for n, w in enumerate(weights)]
    for n in (0, 2):
        w_copies[n].start()

    bar = pltpu.get_barrier_semaphore()

    def greet(to):
        pl.semaphore_signal(bar, inc=1, device_id=to, device_id_type=MESH)

    def x_core(k):
        g = lax.rem(x * 2 + c + k, 2 * nx)
        return g // 2, lax.rem(g, 2)

    def greet_x(k):
        xo, co_ = x_core(k)
        greet(dev(z, y, co_, xo))

    loop(1, 2 * nx, greet_x)
    loop(1, ny, lambda k: greet(dev(z, lax.rem(y + k, ny), c, x)))
    loop(1, nz, lambda k: greet(dev(lax.rem(z + k, nz), y, c, x)))

    def norm_rows(s):
        xn[block(s, D.sites), :] = normed(a_ref[s].astype(F32), g1_ref[...].reshape(1, WIDTH))

    loop(0, D.chains, norm_rows)

    def project(m, h):
        w = jnp.concatenate(
            [w_buf[m, :, (g * hx + h) * HEAD : (g * hx + h + 1) * HEAD] for g in range(nx)], axis=-1
        )
        t = jnp.dot(xn[...], w, preferred_element_type=F32).astype(BF)
        for g in range(nx):
            qkv_s[m, h, g] = jnp.concatenate(
                [
                    t[s * D.sites : (s + 1) * D.sites, g * HEAD : (g + 1) * HEAD]
                    for s in range(D.chains)
                ],
                axis=-1,
            )

    my_sites = block(x, D.sites)
    my_part = block(x, D.psites)

    class Cross:
        def __init__(self, m, h, r=None):
            self.sem = m * hx + h if r is None else (2 + r) * hx + h
            if r is None:
                self.dst = kv_r.at[m, h, my_sites, :]
                self.size = kv_r.at[m, h, pl.ds(0, (nx - 1) * D.sites), :]
                self.src = lambda g: qkv_s.at[m, h, g]
            else:
                self.dst = q_r.at[r, h, my_part, :]
                self.size = q_r.at[r, h, pl.ds(0, (nx - 1) * D.psites), :]
                self.src = lambda g: qkv_s.at[2, h, g, pl.ds(r * D.psites, D.psites), :]

        def copy(self, k):
            xo = lax.rem(x + k, nx)
            return remote(
                self.src(xo), self.dst, x_ss.at[self.sem], x_rs.at[self.sem], dev(z, y, c, xo)
            )

        def keep(self):
            return pltpu.make_async_copy(self.src(x), self.dst, x_ls.at[self.sem])

        def start(self):
            loop(1, nx, lambda k: self.copy(k).start())
            self.keep().start()

        def wait(self):
            self.keep().wait()
            drain(self.size, x_ss.at[self.sem], x_rs.at[self.sem])

    scale = 1.0 / (math.sqrt(HEAD) * math.sqrt(D.total_seqs))
    own_half, far_half = block(c, D.half), block(other, D.half)

    def c_copy(r, h):
        return remote(l_send.at[r, h], l_recv.at[r, h], c_ss.at[r, h], c_rs.at[r, h], sibling)

    def logits(r, h):
        if r == 0:
            Cross(0, h).wait()
        Cross(2, h, r).wait()
        far = lax.dot_general(q_r[r, h, far_half, :], kv_r[0, h], NT, preferred_element_type=F32)
        l_send[r, h] = (far * scale).astype(BF)
        c_copy(r, h).start()
        own = lax.dot_general(q_r[r, h, own_half, :], kv_r[0, h], NT, preferred_element_type=F32)
        l_own[r, h] = own * scale

    def y_copy(r, h, k):
        yo = lax.rem(y + k, ny)
        return remote(
            y_send.at[r, h, block(yo, D.yrows), :],
            y_recv.at[r, h, y],
            y_ss.at[r, h],
            y_rs.at[r, h],
            dev(z, yo, c, x),
        )

    def core_sum(r, h):
        c_copy(r, h).wait()
        total = l_own[r, h] + l_recv[r, h].astype(F32)
        l_own[r, h] = total
        y_send[r, h] = total.astype(BF)
        loop(1, ny, lambda k: y_copy(r, h, k).start())

    zr, slabs = D.zrows, D.total_sites // LANES
    zt = zr * slabs

    def fold(rows):
        n = rows.shape[0] // zr
        return jnp.concatenate(
            [
                rows[i * zr : (i + 1) * zr, j * LANES : (j + 1) * LANES]
                for i in range(n)
                for j in range(slabs)
            ],
            axis=0,
        )

    def unfold(tiles):
        n = tiles.shape[0] // zt
        return jnp.concatenate(
            [
                jnp.concatenate(
                    [tiles[i * zt + j * zr : i * zt + (j + 1) * zr] for i in range(n)], axis=0
                )
                for j in range(slabs)
            ],
            axis=1,
        )

    z_size = pl.ds(0, (nz - 1) * zt)

    def z_copy(r, h, k):
        zo = lax.rem(z + turn(k - 1, nz), nz)
        return remote(
            z_send.at[r, h, block(zo, zt), :],
            z_recv.at[r, h, block(z, zt), :],
            z_ss.at[r, h],
            z_rs.at[r, h],
            dev(zo, y, c, x),
        )

    def y_sum(r, h):
        drain(y_recv.at[r, h, pl.ds(0, ny - 1)], y_ss.at[r, h], y_rs.at[r, h])
        total = l_own[r, h, block(y, D.yrows), :]
        for k in range(1, ny):
            total += y_recv[r, h, lax.rem(y + k, ny)].astype(F32)
        z_send[r, h] = fold(total).astype(BF)
        loop(1, nz, lambda k: z_copy(r, h, k).start())

    def pz_copy(r, h, k):
        zo = lax.rem(z + turn(k - 1, nz), nz)
        return remote(
            p_send.at[r, h], p_z.at[r, h, block(z, zt), :], pz_ss.at[r, h], pz_rs.at[r, h], dev(zo, y, c, x)
        )

    def z_softmax(r, h):
        drain(z_recv.at[r, h, z_size, :], z_ss.at[r, h], z_rs.at[r, h])
        tied = z_send[r, h, block(z, zt), :].astype(F32)
        for k in range(1, nz):
            tied += z_recv[r, h, block(lax.rem(z + k, nz), zt), :].astype(F32)
        prob = fold(softmax(unfold(tied))).astype(BF)
        p_send[r, h] = prob
        loop(1, nz, lambda k: pz_copy(r, h, k).start())
        p_z[r, h, block(z, zt), :] = prob

    py_rows = block(c * ny + y, D.yrows)

    def py_copy(r, h, k):
        yo = lax.rem(y + k, ny)
        place = p_full.at[r, h, py_rows, :]
        return remote(place, place, py_ss.at[r, h], py_rs.at[r, h], dev(z, yo, c, x))

    def gather_z(r, h):
        drain(p_z.at[r, h, z_size, :], pz_ss.at[r, h], pz_rs.at[r, h])
        p_full[r, h, py_rows, :] = unfold(p_z[r, h].astype(F32)).astype(BF)
        loop(1, ny, lambda k: py_copy(r, h, k).start())

    def pc_copy(r, h):
        place = p_full.at[r, h, own_half, :]
        return remote(place, place, pc_ss.at[r, h], pc_rs.at[r, h], sibling)

    def gather_y(r, h):
        drain(p_full.at[r, h, pl.ds(0, (ny - 1) * D.yrows), :], py_ss.at[r, h], py_rs.at[r, h])
        pc_copy(r, h).start()

    def o_rows(xo, core):
        return block(xo * 2 + core, D.csites)

    def o_copy(r, h, k):
        xo, co_ = x_core(k)
        return remote(
            o_send.at[r, h, o_rows(xo, co_), :],
            m_recv.at[r, c, x * hx + h],
            o_ss.at[r, h],
            o_rs.at[r, h],
            dev(z, y, co_, xo),
        )

    def o_local(r, h):
        return pltpu.make_async_copy(
            o_send.at[r, h, o_rows(x, c), :], m_recv.at[r, c, x * hx + h], o_ls.at[r, h]
        )

    def attend(r, h):
        if r == 0:
            Cross(1, h).wait()
        pc_copy(r, h).wait()
        o_send[r, h] = jnp.dot(p_full[r, h], kv_r[1, h], preferred_element_type=F32).astype(BF)
        loop(1, 2 * nx, lambda k: o_copy(r, h, k).start())
        o_local(r, h).start()

    def pack(slabs):
        pieces = [v.reshape(nd, D.pair, LANES) for v in slabs]
        left = jnp.concatenate(pieces[: SLABS // 2], axis=-1)
        right = jnp.concatenate(pieces[SLABS // 2 :], axis=-1)
        return jnp.concatenate([left, right], axis=1).astype(BF).reshape(2 * D.col_len, WIDTH // 2)

    def unpack(packed):
        t = packed.reshape(nd, 2 * D.pair, WIDTH // 2).astype(F32)
        both = jnp.concatenate([t[:, : D.pair], t[:, D.pair :]], axis=-1)
        return both.reshape(D.col_len, WIDTH)

    def d_copies(r, src, dst, ss, rs, ls):
        def copy(k):
            j = nz - 1 - (k - 1) // ny
            dz = turn((k - 1) // ny, nz)
            dy = lax.rem(k - 1, ny) + jnp.where(j == 0, 1, 0)
            p = lax.rem(z + dz, nz) * ny + lax.rem(y + dy, ny)
            return remote(
                src.at[r, block(p, 2 * D.pair), :], dst.at[r, block(d, 2 * D.pair), :], ss.at[r], rs.at[r], dev_d(p)
            )

        mine = block(d, 2 * D.pair)
        keep = pltpu.make_async_copy(src.at[r, mine, :], dst.at[r, mine, :], ls.at[r])
        return copy, keep

    def d_start(r, *refs):
        copy, keep = d_copies(r, *refs)
        loop(1, nd, lambda k: copy(k).start())
        keep.start()

    def d_wait(r, src, dst, ss, rs, ls):
        d_copies(r, src, dst, ss, rs, ls)[1].wait()
        drain(dst.at[r, pl.ds(0, (nd - 1) * 2 * D.pair), :], ss.at[r], rs.at[r])

    into = (c_send, c_recv, i_ss, i_rs, i_ls)
    back = (r_send, r_recv, b_ss, b_rs, b_ls)

    def a_rows(r, core):
        return block(r * 2 + core, D.csites)

    def residual_copies():
        copies = []
        for r in range(D.parts):
            keep = pltpu.make_async_copy(a_ref.at[:, a_rows(r, c), :], a_res.at[r, c], a_ls.at[r])
            swap = remote(a_ref.at[:, a_rows(r, other), :], a_res.at[r, c], a_ss.at[r], a_rs.at[r], sibling)
            keep.start()
            swap.start()
            copies.append((keep, swap))
        return copies

    def after_row(r):
        for h in range(hx):
            o_local(r, h).wait()
            drain(o_send.at[r, h, pl.ds(0, (2 * nx - 1) * D.csites), :], o_ss.at[r, h], o_rs.at[r, h])
        for copy in a_copies[r]:
            copy.wait()
        for cc in range(2):
            for s in range(D.chains):
                n = cc * D.chains + s
                mix[n * D.csites : (n + 1) * D.csites, :] = jnp.concatenate(
                    [m_recv[r, cc, h, :, s * HEAD : (s + 1) * HEAD] for h in range(HEADS)], axis=-1
                )

        def mixing(cb):
            cols = block(cb, 256)
            inc = jnp.dot(mix[...], w_buf[3, :, cols], preferred_element_type=F32)
            for cc in range(2):
                for s in range(D.chains):
                    n = cc * D.chains + s
                    after = a_res[r, cc, s, :, cols].astype(F32) + inc[n * D.csites : (n + 1) * D.csites]
                    for j in range(2):
                        c_f32[cb * 2 + j, pl.ds(n, D.csites, stride=D.pair), :] = after[
                            :, j * LANES : (j + 1) * LANES
                        ]

        loop(0, WIDTH // 256, mixing)
        c_send[r] = pack([c_f32[j] for j in range(SLABS)])
        d_start(r, *into)

    col_scale = 1.0 / math.sqrt(HEAD)
    lane = lax.broadcasted_iota(jnp.int32, (1, 2 * HEAD), 1)

    def column(r):
        d_wait(r, *into)
        wide = unpack(c_recv[r])
        wide_buf[...] = wide
        cn[...] = normed(wide, g2_ref[...].reshape(1, WIDTH))
        for m in range(3):
            c_qkv[m] = jnp.dot(cn[...], w_buf[4 + m], preferred_element_type=F32).astype(BF)

        def two_heads(p):
            cols = block(p, 2 * HEAD)
            q, k, v = c_qkv[0, :, cols], c_qkv[1, :, cols], c_qkv[2, :, cols]
            zero = jnp.zeros_like(k)
            mixed = None
            for side in range(2):
                mine = (lane < HEAD) if side == 0 else (lane >= HEAD)
                scores = lax.dot_general(
                    q, jnp.where(mine, k, zero), NT, preferred_element_type=F32
                )
                prob = softmax(scores * col_scale).astype(BF)
                part = jnp.dot(prob, jnp.where(mine, v, zero), preferred_element_type=F32)
                mixed = part if mixed is None else mixed + part
            c_mix[:, cols] = mixed.astype(BF)

        loop(0, HEADS // 2, two_heads)
        change = jnp.dot(c_mix[...], w_buf[7], preferred_element_type=F32)
        total = wide_buf[...] + change
        r_send[r] = pack([total[:, j * LANES : (j + 1) * LANES] for j in range(SLABS)])
        d_start(r, *back)

    def f_copy(r):
        return remote(f_send.at[r], out_ref.at[:, a_rows(r, c), :], f_ss.at[r], f_rs.at[r], sibling)

    def finish(r):
        d_wait(r, *back)
        total = unpack(r_recv[r])
        for j in range(SLABS):
            c_f32[j] = total[:, j * LANES : (j + 1) * LANES]

        def chain_rows(s):
            rows = pl.ds(s, D.csites, stride=D.pair)
            return jnp.concatenate([c_f32[j, rows, :] for j in range(SLABS)], axis=1).astype(BF)

        for s in range(D.chains):
            f_send[r, s] = chain_rows(other * D.chains + s)
        f_copy(r).start()
        for s in range(D.chains):
            out_ref[s, a_rows(r, c), :] = chain_rows(c * D.chains + s)

    for m in (0, 2):
        w_copies[m].wait()
    for n in (1, 3, 4, 5, 6, 7):
        w_copies[n].start()

    def first(h):
        Cross(0, h).start()
        Cross(2, h, 0).start()

    project(0, 0)
    project(2, 0)
    pl.semaphore_wait(bar, 2 * nx - 1 + ny - 1 + nz - 1)
    first(0)
    project(0, 1)
    project(2, 1)
    first(1)
    project(0, 2)
    project(2, 2)
    a_copies = residual_copies()
    w_copies[1].wait()
    for h in range(hx):
        project(1, h)

    def queries(h):
        Cross(2, h, 1).start()

    def values(h):
        Cross(1, h).start()

    def weights_in():
        for n in range(3, 8):
            w_copies[n].wait()

    plan = (
        (logits, 0, 0), (first, 2), (core_sum, 0, 0), (logits, 0, 1), (queries, 0), (queries, 1), (queries, 2),
        (core_sum, 0, 1), (y_sum, 0, 0), (logits, 0, 2), (values, 0), (values, 1), (values, 2),
        (core_sum, 0, 2), (y_sum, 0, 1), (z_softmax, 0, 0), (logits, 1, 0), (core_sum, 1, 0), (y_sum, 0, 2),
        (z_softmax, 0, 1), (gather_z, 0, 0), (logits, 1, 1), (core_sum, 1, 1), (y_sum, 1, 0), (z_softmax, 0, 2),
        (gather_z, 0, 1), (gather_y, 0, 0), (logits, 1, 2), (core_sum, 1, 2), (y_sum, 1, 1), (attend, 0, 0),
        (z_softmax, 1, 0), (gather_z, 0, 2), (gather_y, 0, 1), (y_sum, 1, 2), (attend, 0, 1), (z_softmax, 1, 1),
        (gather_z, 1, 0), (gather_y, 0, 2), (weights_in,), (attend, 0, 2), (z_softmax, 1, 2), (gather_z, 1, 1),
        (gather_y, 1, 0), (attend, 1, 0), (gather_z, 1, 2), (after_row, 0), (gather_y, 1, 1), (attend, 1, 1),
        (gather_y, 1, 2), (attend, 1, 2), (after_row, 1), (column, 0), (column, 1), (finish, 0), (finish, 1),
    )
    for step, *args in plan:
        step(*args)
    f_copy(0).wait()
    f_copy(1).wait()


def on_device(D, a, g1, wq, wk, wv, wo, g2, cq, ck, cv, co):
    vmem = pl.BlockSpec(memory_space=pltpu.VMEM)
    hbm = pl.BlockSpec(memory_space=pl.ANY)
    sites, N, H, L = D.total_sites, D.parts, D.hx, D.chains * HEAD
    bf = lambda *shape: pltpu.VMEM(shape, BF)
    f32 = lambda *shape: pltpu.VMEM(shape, F32)
    sem = lambda *shape: pltpu.SemaphoreType.DMA(shape)
    scratch = dict(
        w_buf=bf(8, WIDTH, WIDTH),
        xn=bf(D.rows, WIDTH),
        qkv_s=bf(3, D.hx, D.nx, D.sites, L),
        kv_r=bf(2, H, sites, L),
        q_r=bf(N, H, D.prows, L),
        l_own=f32(N, H, D.half, sites),
        l_send=bf(N, H, D.half, sites),
        l_recv=bf(N, H, D.half, sites),
        y_send=bf(N, H, D.half, sites),
        y_recv=bf(N, H, D.ny, D.yrows, sites),
        z_send=bf(N, H, D.yrows * sites // LANES, LANES),
        z_recv=bf(N, H, D.yrows * sites // LANES, LANES),
        p_send=bf(N, H, D.zrows * sites // LANES, LANES),
        p_z=bf(N, H, D.yrows * sites // LANES, LANES),
        p_full=bf(N, H, D.prows, sites),
        o_send=bf(N, H, D.prows, L),
        m_recv=bf(N, 2, HEADS, D.csites, L),
        a_res=bf(N, 2, D.chains, D.csites, WIDTH),
        mix=bf(D.pair * D.csites, WIDTH),
        c_f32=f32(SLABS, D.col_len, LANES),
        c_send=bf(N, 2 * D.col_len, WIDTH // 2),
        c_recv=bf(N, 2 * D.col_len, WIDTH // 2),
        wide_buf=f32(D.col_len, WIDTH),
        cn=bf(D.col_len, WIDTH),
        c_qkv=bf(3, D.col_len, WIDTH),
        c_mix=bf(D.col_len, WIDTH),
        r_send=bf(N, 2 * D.col_len, WIDTH // 2),
        r_recv=bf(N, 2 * D.col_len, WIDTH // 2),
        f_send=bf(N, D.chains, D.csites, WIDTH),
        w_sem=sem(8),
        x_ss=sem((2 + N) * H), x_rs=sem((2 + N) * H), x_ls=sem((2 + N) * H),
        a_ls=sem(N), a_ss=sem(N), a_rs=sem(N),
        c_ss=sem(N, H), c_rs=sem(N, H), y_ss=sem(N, H), y_rs=sem(N, H), z_ss=sem(N, H), z_rs=sem(N, H),
        pz_ss=sem(N, H), pz_rs=sem(N, H), py_ss=sem(N, H), py_rs=sem(N, H), pc_ss=sem(N, H), pc_rs=sem(N, H),
        o_ss=sem(N, H), o_rs=sem(N, H), o_ls=sem(N, H),
        i_ss=sem(N), i_rs=sem(N), i_ls=sem(N), b_ss=sem(N), b_rs=sem(N), b_ls=sem(N),
        f_ss=sem(N), f_rs=sem(N),
    )
    flops = 2 * (8 * D.rows * WIDTH * WIDTH + 2 * D.hx * sites * sites * L)
    return pl.pallas_call(
        functools.partial(layer, D),
        out_shape=jax.ShapeDtypeStruct(a.shape, a.dtype),
        in_specs=[vmem] * 3 + [hbm] * 8,
        out_specs=vmem,
        scratch_shapes=list(scratch.values()),
        compiler_params=pltpu.CompilerParams(
            collective_id=0, has_side_effects=True, vmem_limit_bytes=60 * 2**20
        ),
        cost_estimate=pl.CostEstimate(flops=flops, bytes_accessed=12 * 2**20, transcendentals=2**21),
        name="msa_layer",
    )(a, g1, g2, wq, wk, wv, wo, cq, ck, cv, co)


def solution(mesh):
    nseq, nx = mesh.shape["seq"], mesh.shape["res"]
    ny = 4

    def step(a, *rest):
        D = Dims(nseq, nx, ny, a.shape[0], a.shape[1])
        return on_device(D, a, *rest)

    in_specs = (P("seq", "res", None),) + (P(),) * 10
    return jax.shard_map(
        step, mesh=mesh, in_specs=in_specs, out_specs=P("seq", "res", None), check_vma=False
    )
```

```python
import functools
import math

import jax
import jax.numpy as jnp
from jax import lax
from jax.experimental import pallas as pl
from jax.experimental.pallas import tpu as pltpu
from jax.sharding import PartitionSpec as P

MESH = pl.DeviceIdType.MESH
HEADS = 12
HEAD = 64
WIDTH = HEADS * HEAD
LANES = 128
SLABS = WIDTH // LANES
BF = jnp.bfloat16
F32 = jnp.float32
NT = (((1,), (1,)), ((), ()))


class Dims:
    def __init__(self, nseq, nx, ny, chains, sites):
        self.nx, self.ny = nx, ny
        self.nz = nseq // (2 * ny)
        self.nd = self.ny * self.nz
        self.chains, self.sites = chains, sites
        self.rows = chains * sites
        self.hx = HEADS // nx
        self.total_sites = sites * nx
        self.parts = sites // (2 * self.nd)
        self.psites = sites // self.parts
        self.csites = self.psites // 2
        self.prows = self.psites * nx
        self.half = self.prows // 2
        self.yrows = self.half // ny
        self.zrows = self.yrows // self.nz
        self.pair = 2 * chains
        self.col_len = self.nd * self.pair
        self.total_seqs = nseq * chains
        assert self.csites == self.nd and self.pair == 8 and self.zrows == 4


def normed(wide, gain):
    center = wide - jnp.mean(wide, axis=-1, keepdims=True)
    spread = jnp.mean(center * center, axis=-1, keepdims=True)
    return (center * lax.rsqrt(spread + 1e-05) * gain).astype(BF)


def softmax(scores):
    top = jnp.max(scores, axis=-1, keepdims=True)
    e = jnp.exp(scores - top)
    return e / jnp.sum(e, axis=-1, keepdims=True)


def layer(
    D,
    a_hbm, g1_ref, g2_ref,
    wq, wk, wv, wo, cq, ck, cv, co,
    out_ref,
    a_ref, out_v, w_buf, xn, qkv_s, kv_r, q_r, l_own, l_send, l_recv, y_send, y_recv, z_send, z_recv,
    p_send, p_z, p_full, o_send, m_recv, wo_buf, acc, a_res, mix, c_f32, c_send, c_recv, wide_buf, cn, c_qkv, c_mix,
    r_send, r_recv, f_send,
    w_sem, wo_sem, x_ss, x_rs, x_ls, a_ls, a_ss, a_rs, c_ss, c_rs, y_ss, y_rs, z_ss, z_rs, pz_ss, pz_rs, py_ss, py_rs,
    pc_ss, pc_rs, o_ss, o_rs, o_ls, i_ss, i_rs, i_ls, b_ss, b_rs, b_ls, f_ss, f_rs, out_sem,
):
    nx, ny, nz, nd, hx = D.nx, D.ny, D.nz, D.nd, D.hx
    seq, x = lax.axis_index("seq"), lax.axis_index("res")
    c = lax.rem(seq, 2)
    d = seq // 2
    y = lax.rem(d, ny)
    z = d // ny
    other = 1 - c

    def dev(z_, y_, c_, x_):
        return ((z_ * ny + y_) * 2 + c_, x_)

    def dev_d(p):
        return dev(p // ny, lax.rem(p, ny), c, x)

    sibling = dev(z, y, other, x)

    def remote(src, dst, ss, rs, to):
        return pltpu.make_async_remote_copy(
            src_ref=src, dst_ref=dst, send_sem=ss, recv_sem=rs, device_id=to, device_id_type=MESH
        )

    def loop(lo, hi, body):
        def step(k, carry):
            body(k)
            return carry

        lax.fori_loop(lo, hi, step, 0)

    def drain(ref, *sems):
        for sem in sems:
            pltpu.make_async_copy(ref, ref, sem).wait()

    def block(i, n):
        return pl.ds(pl.multiple_of(i * n, n), n)

    def turn(i, n):
        j = n - 1 - i
        far = (j + 1) // 2
        return lax.rem(far + (n - 2 * far) * lax.rem(j + 1, 2), n)

    weights = (wk, wv, wq, cq, ck, cv, co)
    wo_copies = [pltpu.make_async_copy(wo.at[:, h], wo_buf.at[h], wo_sem.at[h]) for h in range(hx)]
    w_copies = [pltpu.make_async_copy(w, w_buf.at[n], w_sem.at[n]) for n, w in enumerate(weights)]
    a_in = pltpu.make_async_copy(a_hbm, a_ref, out_sem.at[D.parts])
    a_in.start()
    for n in (0, 2):
        w_copies[n].start()

    bar = pltpu.get_barrier_semaphore()

    def greet(to):
        pl.semaphore_signal(bar, inc=1, device_id=to, device_id_type=MESH)

    def x_core(k):
        xo = lax.rem(x + turn((k - 1) // 2, nx), nx)
        side = lax.rem(k - 1, 2) + jnp.where(k == 2 * nx - 1, 1, 0)
        return xo, lax.rem(c + side, 2)

    def greet_x(k):
        xo, co_ = x_core(k)
        greet(dev(z, y, co_, xo))

    loop(1, 2 * nx, greet_x)
    loop(1, ny, lambda k: greet(dev(z, lax.rem(y + k, ny), c, x)))
    loop(1, nz, lambda k: greet(dev(lax.rem(z + k, nz), y, c, x)))

    a_in.wait()
    def norm_rows(s):
        xn[block(s, D.sites), :] = normed(a_ref[s].astype(F32), g1_ref[...].reshape(1, WIDTH))

    loop(0, D.chains, norm_rows)

    def project(m, h):
        w = jnp.concatenate(
            [w_buf[m, :, (g * hx + h) * HEAD : (g * hx + h + 1) * HEAD] for g in range(nx)], axis=-1
        )
        t = jnp.dot(xn[...], w, preferred_element_type=F32).astype(BF)
        for g in range(nx):
            qkv_s[m, h, g] = jnp.concatenate(
                [
                    t[s * D.sites : (s + 1) * D.sites, g * HEAD : (g + 1) * HEAD]
                    for s in range(D.chains)
                ],
                axis=-1,
            )

    my_sites = block(x, D.sites)
    my_part = block(x, D.psites)

    class Cross:
        def __init__(self, m, h, r=None):
            self.sem = m * hx + h if r is None else (2 + r) * hx + h
            if r is None:
                self.dst = kv_r.at[m, h, my_sites, :]
                self.size = kv_r.at[m, h, pl.ds(0, (nx - 1) * D.sites), :]
                self.src = lambda g: qkv_s.at[m, h, g]
            else:
                self.dst = q_r.at[r, h, my_part, :]
                self.size = q_r.at[r, h, pl.ds(0, (nx - 1) * D.psites), :]
                self.src = lambda g: qkv_s.at[2, h, g, pl.ds(r * D.psites, D.psites), :]

        def copy(self, k):
            xo = lax.rem(x + turn(k - 1, nx), nx)
            return remote(
                self.src(xo), self.dst, x_ss.at[self.sem], x_rs.at[self.sem], dev(z, y, c, xo)
            )

        def keep(self):
            return pltpu.make_async_copy(self.src(x), self.dst, x_ls.at[self.sem])

        def start(self):
            loop(1, nx, lambda k: self.copy(k).start())
            self.keep().start()

        def wait(self):
            self.keep().wait()
            drain(self.size, x_ss.at[self.sem], x_rs.at[self.sem])

    scale = 1.0 / (math.sqrt(HEAD) * math.sqrt(D.total_seqs))
    own_half, far_half = block(c, D.half), block(other, D.half)

    def c_copy(r, h):
        return remote(l_send.at[r, h], l_recv.at[r, h], c_ss.at[r, h], c_rs.at[r, h], sibling)

    def logits(r, h):
        if r == 0:
            Cross(0, h).wait()
        Cross(2, h, r).wait()
        far = lax.dot_general(q_r[r, h, far_half, :], kv_r[0, h], NT, preferred_element_type=F32)
        l_send[r, h] = (far * scale).astype(BF)
        c_copy(r, h).start()
        own = lax.dot_general(q_r[r, h, own_half, :], kv_r[0, h], NT, preferred_element_type=F32)
        l_own[r, h] = own * scale

    def y_copy(r, h, k):
        yo = lax.rem(y + turn(k - 1, ny), ny)
        return remote(
            y_send.at[r, h, block(yo, D.yrows), :],
            y_recv.at[r, h, y],
            y_ss.at[r, h],
            y_rs.at[r, h],
            dev(z, yo, c, x),
        )

    def core_sum(r, h):
        c_copy(r, h).wait()
        total = l_own[r, h] + l_recv[r, h].astype(F32)
        l_own[r, h] = total
        y_send[r, h] = total.astype(BF)
        loop(1, ny, lambda k: y_copy(r, h, k).start())

    zr, slabs = D.zrows, D.total_sites // LANES
    zt = zr * slabs

    def fold(rows):
        n = rows.shape[0] // zr
        return jnp.concatenate(
            [
                rows[i * zr : (i + 1) * zr, j * LANES : (j + 1) * LANES]
                for i in range(n)
                for j in range(slabs)
            ],
            axis=0,
        )

    def unfold(tiles):
        n = tiles.shape[0] // zt
        return jnp.concatenate(
            [
                jnp.concatenate(
                    [tiles[i * zt + j * zr : i * zt + (j + 1) * zr] for i in range(n)], axis=0
                )
                for j in range(slabs)
            ],
            axis=1,
        )

    z_size = pl.ds(0, (nz - 1) * zt)

    def z_copy(r, h, k):
        zo = lax.rem(z + turn(k - 1, nz), nz)
        return remote(
            z_send.at[r, h, block(zo, zt), :],
            z_recv.at[r, h, block(z, zt), :],
            z_ss.at[r, h],
            z_rs.at[r, h],
            dev(zo, y, c, x),
        )

    def y_sum(r, h):
        drain(y_recv.at[r, h, pl.ds(0, ny - 1)], y_ss.at[r, h], y_rs.at[r, h])
        total = l_own[r, h, block(y, D.yrows), :]
        for k in range(1, ny):
            total += y_recv[r, h, lax.rem(y + k, ny)].astype(F32)
        z_send[r, h] = fold(total).astype(BF)
        loop(1, nz, lambda k: z_copy(r, h, k).start())

    def pz_copy(r, h, k):
        zo = lax.rem(z + turn(k - 1, nz), nz)
        return remote(
            p_send.at[r, h], p_z.at[r, h, block(z, zt), :], pz_ss.at[r, h], pz_rs.at[r, h], dev(zo, y, c, x)
        )

    def z_softmax(r, h):
        drain(z_recv.at[r, h, z_size, :], z_ss.at[r, h], z_rs.at[r, h])
        tied = z_send[r, h, block(z, zt), :].astype(F32)
        for k in range(1, nz):
            tied += z_recv[r, h, block(lax.rem(z + k, nz), zt), :].astype(F32)
        prob = fold(softmax(unfold(tied))).astype(BF)
        p_send[r, h] = prob
        loop(1, nz, lambda k: pz_copy(r, h, k).start())
        p_z[r, h, block(z, zt), :] = prob

    py_rows = block(c * ny + y, D.yrows)

    def py_copy(r, h, k):
        yo = lax.rem(y + turn(k - 1, ny), ny)
        place = p_full.at[r, h, py_rows, :]
        return remote(place, place, py_ss.at[r, h], py_rs.at[r, h], dev(z, yo, c, x))

    def gather_z(r, h):
        drain(p_z.at[r, h, z_size, :], pz_ss.at[r, h], pz_rs.at[r, h])
        p_full[r, h, py_rows, :] = unfold(p_z[r, h].astype(F32)).astype(BF)
        loop(1, ny, lambda k: py_copy(r, h, k).start())

    def pc_copy(r, h):
        place = p_full.at[r, h, own_half, :]
        return remote(place, place, pc_ss.at[r, h], pc_rs.at[r, h], sibling)

    def gather_y(r, h):
        drain(p_full.at[r, h, pl.ds(0, (ny - 1) * D.yrows), :], py_ss.at[r, h], py_rs.at[r, h])
        pc_copy(r, h).start()

    def o_rows(xo, core):
        return block(xo * 2 + core, D.csites)

    def o_copy(r, h, k):
        xo, co_ = x_core(k)
        return remote(
            o_send.at[r, h, o_rows(xo, co_), :],
            m_recv.at[r, c, h, x],
            o_ss.at[r, h],
            o_rs.at[r, h],
            dev(z, y, co_, xo),
        )

    def o_local(r, h):
        return pltpu.make_async_copy(
            o_send.at[r, h, o_rows(x, c), :], m_recv.at[r, c, h, x], o_ls.at[r, h]
        )

    def attend(r, h):
        if r == 0:
            Cross(1, h).wait()
        pc_copy(r, h).wait()
        o_send[r, h] = jnp.dot(p_full[r, h], kv_r[1, h], preferred_element_type=F32).astype(BF)
        loop(1, 2 * nx, lambda k: o_copy(r, h, k).start())
        o_local(r, h).start()

    def pack(slabs):
        pieces = [v.reshape(nd, D.pair, LANES) for v in slabs]
        left = jnp.concatenate(pieces[: SLABS // 2], axis=-1)
        right = jnp.concatenate(pieces[SLABS // 2 :], axis=-1)
        return jnp.concatenate([left, right], axis=1).astype(BF).reshape(2 * D.col_len, WIDTH // 2)

    def unpack(packed):
        t = packed.reshape(nd, 2 * D.pair, WIDTH // 2).astype(F32)
        both = jnp.concatenate([t[:, : D.pair], t[:, D.pair :]], axis=-1)
        return both.reshape(D.col_len, WIDTH)

    def d_copies(r, src, dst, ss, rs, ls):
        def copy(k):
            j = nz - 1 - (k - 1) // ny
            dz = turn((k - 1) // ny, nz)
            dy = lax.rem(k - 1, ny) + jnp.where(j == 0, 1, 0)
            p = lax.rem(z + dz, nz) * ny + lax.rem(y + dy, ny)
            return remote(
                src.at[r, block(p, 2 * D.pair), :], dst.at[r, block(d, 2 * D.pair), :], ss.at[r], rs.at[r], dev_d(p)
            )

        mine = block(d, 2 * D.pair)
        keep = pltpu.make_async_copy(src.at[r, mine, :], dst.at[r, mine, :], ls.at[r])
        return copy, keep

    def d_start(r, *refs):
        copy, keep = d_copies(r, *refs)
        loop(1, nd, lambda k: copy(k).start())
        keep.start()

    def d_wait(r, src, dst, ss, rs, ls):
        d_copies(r, src, dst, ss, rs, ls)[1].wait()
        drain(dst.at[r, pl.ds(0, (nd - 1) * 2 * D.pair), :], ss.at[r], rs.at[r])

    into = (c_send, c_recv, i_ss, i_rs, i_ls)
    back = (r_send, r_recv, b_ss, b_rs, b_ls)

    def a_rows(r, core):
        return block(r * 2 + core, D.csites)

    def residual_copies():
        copies = []
        for r in range(D.parts):
            keep = pltpu.make_async_copy(a_ref.at[:, a_rows(r, c), :], a_res.at[r, c], a_ls.at[r])
            swap = remote(a_ref.at[:, a_rows(r, other), :], a_res.at[r, c], a_ss.at[r], a_rs.at[r], sibling)
            keep.start()
            swap.start()
            copies.append((keep, swap))
        return copies

    def mixing(r, h):
        o_local(r, h).wait()
        drain(o_send.at[r, h, pl.ds(0, (2 * nx - 1) * D.csites), :], o_ss.at[r, h], o_rs.at[r, h])
        chains = [(cc, s) for cc in range(2) for s in range(D.chains)]
        for n, (cc, s) in enumerate(chains):
            mix[n * D.csites : (n + 1) * D.csites, :] = jnp.concatenate(
                [m_recv[r, cc, h, g, :, s * HEAD : (s + 1) * HEAD] for g in range(nx)], axis=-1
            )
        if h == 0:
            for copy in a_copies[r]:
                copy.wait()
            for n, (cc, s) in enumerate(chains):
                acc[r, n * D.csites : (n + 1) * D.csites, :] = a_res[r, cc, s].astype(F32)

        def columns(cb):
            cols = block(cb, 256)
            part = wo_buf[h, :, :, cols].reshape(nx * HEAD, 256)
            total = acc[r, :, cols] + jnp.dot(mix[...], part, preferred_element_type=F32)
            if h < hx - 1:
                acc[r, :, cols] = total
            else:
                for n in range(D.pair):
                    for j in range(2):
                        c_f32[cb * 2 + j, pl.ds(n, D.csites, stride=D.pair), :] = total[
                            n * D.csites : (n + 1) * D.csites, j * LANES : (j + 1) * LANES
                        ]

        loop(0, WIDTH // 256, columns)

    def after_row(r):
        mixing(r, hx - 1)
        c_send[r] = pack([c_f32[j] for j in range(SLABS)])
        d_start(r, *into)

    col_scale = 1.0 / math.sqrt(HEAD)
    lane = lax.broadcasted_iota(jnp.int32, (1, 2 * HEAD), 1)

    def column(r):
        d_wait(r, *into)
        wide = unpack(c_recv[r])
        wide_buf[...] = wide
        cn[...] = normed(wide, g2_ref[...].reshape(1, WIDTH))
        for m in range(3):
            c_qkv[m] = jnp.dot(cn[...], w_buf[3 + m], preferred_element_type=F32).astype(BF)

        def two_heads(p):
            cols = block(p, 2 * HEAD)
            q, k, v = c_qkv[0, :, cols], c_qkv[1, :, cols], c_qkv[2, :, cols]
            zero = jnp.zeros_like(k)
            mixed = None
            for side in range(2):
                mine = (lane < HEAD) if side == 0 else (lane >= HEAD)
                scores = lax.dot_general(
                    q, jnp.where(mine, k, zero), NT, preferred_element_type=F32
                )
                prob = softmax(scores * col_scale).astype(BF)
                part = jnp.dot(prob, jnp.where(mine, v, zero), preferred_element_type=F32)
                mixed = part if mixed is None else mixed + part
            c_mix[:, cols] = mixed.astype(BF)

        loop(0, HEADS // 2, two_heads)
        change = jnp.dot(c_mix[...], w_buf[6], preferred_element_type=F32)
        total = wide_buf[...] + change
        r_send[r] = pack([total[:, j * LANES : (j + 1) * LANES] for j in range(SLABS)])
        d_start(r, *back)

    def f_copy(r):
        return remote(f_send.at[r], out_ref.at[:, a_rows(r, c), :], f_ss.at[r], f_rs.at[r], sibling)

    def out_copy(r):
        return pltpu.make_async_copy(out_v.at[r], out_ref.at[:, a_rows(r, c), :], out_sem.at[r])

    def finish(r):
        d_wait(r, *back)
        total = unpack(r_recv[r])
        for j in range(SLABS):
            c_f32[j] = total[:, j * LANES : (j + 1) * LANES]

        def chain_rows(s):
            rows = pl.ds(s, D.csites, stride=D.pair)
            return jnp.concatenate([c_f32[j, rows, :] for j in range(SLABS)], axis=1).astype(BF)

        for s in range(D.chains):
            f_send[r, s] = chain_rows(other * D.chains + s)
        f_copy(r).start()
        for s in range(D.chains):
            out_v[r, s] = chain_rows(c * D.chains + s)
        out_copy(r).start()

    for m in (0, 2):
        w_copies[m].wait()
    for n in (1, 3, 4, 5, 6):
        w_copies[n].start()
    for copy in wo_copies:
        copy.start()

    def first(h):
        Cross(0, h).start()
        Cross(2, h, 0).start()

    project(0, 0)
    project(2, 0)
    pl.semaphore_wait(bar, 2 * nx - 1 + ny - 1 + nz - 1)
    first(0)
    project(0, 1)
    project(2, 1)
    first(1)
    project(0, 2)
    project(2, 2)
    a_copies = residual_copies()
    w_copies[1].wait()
    for h in range(hx):
        project(1, h)

    def queries(h):
        Cross(2, h, 1).start()

    def values(h):
        Cross(1, h).start()

    def weights_in():
        for n in range(3, 7):
            w_copies[n].wait()
        for copy in wo_copies:
            copy.wait()

    plan = (
        (logits, 0, 0), (first, 2), (core_sum, 0, 0), (logits, 0, 1), (queries, 0), (queries, 1), (queries, 2),
        (core_sum, 0, 1), (y_sum, 0, 0), (logits, 0, 2), (values, 0), (values, 1), (values, 2),
        (core_sum, 0, 2), (y_sum, 0, 1), (z_softmax, 0, 0), (logits, 1, 0), (core_sum, 1, 0), (y_sum, 0, 2),
        (z_softmax, 0, 1), (gather_z, 0, 0), (logits, 1, 1), (core_sum, 1, 1), (y_sum, 1, 0), (z_softmax, 0, 2),
        (gather_z, 0, 1), (gather_y, 0, 0), (logits, 1, 2), (core_sum, 1, 2), (y_sum, 1, 1), (attend, 0, 0),
        (z_softmax, 1, 0), (gather_z, 0, 2), (gather_y, 0, 1), (y_sum, 1, 2), (attend, 0, 1), (z_softmax, 1, 1), (weights_in,), (mixing, 0, 0),
        (gather_z, 1, 0), (gather_y, 0, 2), (attend, 0, 2), (z_softmax, 1, 2), (mixing, 0, 1), (gather_z, 1, 1),
        (gather_y, 1, 0), (attend, 1, 0), (gather_z, 1, 2), (after_row, 0), (gather_y, 1, 1), (attend, 1, 1),
        (mixing, 1, 0), (gather_y, 1, 2), (attend, 1, 2), (mixing, 1, 1), (after_row, 1), (column, 0), (column, 1), (finish, 0), (finish, 1),
    )
    for step, *args in plan:
        step(*args)
    for r in range(D.parts):
        f_copy(r).wait()
        out_copy(r).wait()


def on_device(D, a, g1, wq, wk, wv, wo, g2, cq, ck, cv, co):
    vmem = pl.BlockSpec(memory_space=pltpu.VMEM)
    hbm = pl.BlockSpec(memory_space=pl.ANY)
    sites, N, H, L = D.total_sites, D.parts, D.hx, D.chains * HEAD
    bf = lambda *shape: pltpu.VMEM(shape, BF)
    f32 = lambda *shape: pltpu.VMEM(shape, F32)
    sem = lambda *shape: pltpu.SemaphoreType.DMA(shape)
    scratch = dict(
        a_ref=bf(D.chains, D.sites, WIDTH),
        out_v=bf(N, D.chains, D.csites, WIDTH),
        w_buf=bf(7, WIDTH, WIDTH),
        xn=bf(D.rows, WIDTH),
        qkv_s=bf(3, D.hx, D.nx, D.sites, L),
        kv_r=bf(2, H, sites, L),
        q_r=bf(N, H, D.prows, L),
        l_own=f32(N, H, D.half, sites),
        l_send=bf(N, H, D.half, sites),
        l_recv=bf(N, H, D.half, sites),
        y_send=bf(N, H, D.half, sites),
        y_recv=bf(N, H, D.ny, D.yrows, sites),
        z_send=bf(N, H, D.yrows * sites // LANES, LANES),
        z_recv=bf(N, H, D.yrows * sites // LANES, LANES),
        p_send=bf(N, H, D.zrows * sites // LANES, LANES),
        p_z=bf(N, H, D.yrows * sites // LANES, LANES),
        p_full=bf(N, H, D.prows, sites),
        o_send=bf(N, H, D.prows, L),
        m_recv=bf(N, 2, H, D.nx, D.csites, L),
        wo_buf=bf(H, D.nx, HEAD, WIDTH),
        acc=f32(N, D.col_len, WIDTH),
        a_res=bf(N, 2, D.chains, D.csites, WIDTH),
        mix=bf(D.pair * D.csites, L),
        c_f32=f32(SLABS, D.col_len, LANES),
        c_send=bf(N, 2 * D.col_len, WIDTH // 2),
        c_recv=bf(N, 2 * D.col_len, WIDTH // 2),
        wide_buf=f32(D.col_len, WIDTH),
        cn=bf(D.col_len, WIDTH),
        c_qkv=bf(3, D.col_len, WIDTH),
        c_mix=bf(D.col_len, WIDTH),
        r_send=bf(N, 2 * D.col_len, WIDTH // 2),
        r_recv=bf(N, 2 * D.col_len, WIDTH // 2),
        f_send=bf(N, D.chains, D.csites, WIDTH),
        w_sem=sem(7), wo_sem=sem(H),
        x_ss=sem((2 + N) * H), x_rs=sem((2 + N) * H), x_ls=sem((2 + N) * H),
        a_ls=sem(N), a_ss=sem(N), a_rs=sem(N),
        c_ss=sem(N, H), c_rs=sem(N, H), y_ss=sem(N, H), y_rs=sem(N, H), z_ss=sem(N, H), z_rs=sem(N, H),
        pz_ss=sem(N, H), pz_rs=sem(N, H), py_ss=sem(N, H), py_rs=sem(N, H), pc_ss=sem(N, H), pc_rs=sem(N, H),
        o_ss=sem(N, H), o_rs=sem(N, H), o_ls=sem(N, H),
        i_ss=sem(N), i_rs=sem(N), i_ls=sem(N), b_ss=sem(N), b_rs=sem(N), b_ls=sem(N),
        f_ss=sem(N), f_rs=sem(N), out_sem=sem(N + 1),
    )
    flops = 2 * (8 * D.rows * WIDTH * WIDTH + 2 * D.hx * sites * sites * L)
    return pl.pallas_call(
        functools.partial(layer, D),
        out_shape=jax.ShapeDtypeStruct(a.shape, a.dtype),
        in_specs=[hbm] + [vmem] * 2 + [hbm] * 8,
        out_specs=hbm,
        scratch_shapes=list(scratch.values()),
        compiler_params=pltpu.CompilerParams(
            collective_id=0, has_side_effects=True, vmem_limit_bytes=60 * 2**20
        ),
        cost_estimate=pl.CostEstimate(flops=flops, bytes_accessed=12 * 2**20, transcendentals=2**21),
        name="msa_layer",
    )(a, g1, g2, wq, wk, wv, wo.reshape(D.nx, H, HEAD, WIDTH), cq, ck, cv, co)


def solution(mesh):
    nseq, nx = mesh.shape["seq"], mesh.shape["res"]
    ny = 4

    def step(a, *rest):
        D = Dims(nseq, nx, ny, a.shape[0], a.shape[1])
        return on_device(D, a, *rest)

    in_specs = (P("seq", "res", None),) + (P(),) * 10
    return jax.shard_map(
        step, mesh=mesh, in_specs=in_specs, out_specs=P("seq", "res", None), check_vma=False
    )
```

```python
import functools
import math

import jax
import jax.numpy as jnp
from jax import lax
from jax.experimental import pallas as pl
from jax.experimental.pallas import tpu as pltpu
from jax.sharding import PartitionSpec as P

MESH = pl.DeviceIdType.MESH
HEADS = 12
HEAD = 64
WIDTH = HEADS * HEAD
LANES = 128
SLABS = WIDTH // LANES
BF = jnp.bfloat16
F32 = jnp.float32
NT = (((1,), (1,)), ((), ()))


class Dims:
    def __init__(self, nseq, nx, ny, chains, sites):
        self.nx, self.ny = nx, ny
        self.nz = nseq // (2 * ny)
        self.nd = self.ny * self.nz
        self.chains, self.sites = chains, sites
        self.rows = chains * sites
        self.hx = HEADS // nx
        self.total_sites = sites * nx
        self.parts = sites // (2 * self.nd)
        self.psites = sites // self.parts
        self.csites = self.psites // 2
        self.prows = self.psites * nx
        self.half = self.prows // 2
        self.yrows = self.half // ny
        self.zrows = self.yrows // self.nz
        self.pair = 2 * chains
        self.col_len = self.nd * self.pair
        self.total_seqs = nseq * chains
        assert self.csites == self.nd and self.pair == 8 and self.zrows == 4


def normed(wide, gain):
    center = wide - jnp.mean(wide, axis=-1, keepdims=True)
    spread = jnp.mean(center * center, axis=-1, keepdims=True)
    return (center * lax.rsqrt(spread + 1e-05) * gain).astype(BF)


def softmax(scores):
    top = jnp.max(scores, axis=-1, keepdims=True)
    e = jnp.exp(scores - top)
    return e / jnp.sum(e, axis=-1, keepdims=True)


def layer(
    D,
    a_hbm, g1_ref, g2_ref,
    wq, wk, wv, wo, cq, ck, cv, co,
    out_ref,
    a_ref, out_v, w_buf, xn, qkv_s, kv_r, q_r, l_own, l_send, l_recv, y_send, y_recv, z_send, z_recv,
    p_send, p_z, p_full, o_send, m_recv, wo_buf, acc, a_res, mix, c_f32, c_send, c_recv, wide_buf, cn, c_qkv, c_mix,
    r_send, r_recv, f_send,
    w_sem, wo_sem, x_ss, x_rs, x_ls, a_ls, a_ss, a_rs, c_ss, c_rs, y_ss, y_rs, z_ss, z_rs, pz_ss, pz_rs, py_ss, py_rs,
    pc_ss, pc_rs, o_ss, o_rs, o_ls, i_ss, i_rs, i_ls, b_ss, b_rs, b_ls, f_ss, f_rs, out_sem,
):
    nx, ny, nz, nd, hx = D.nx, D.ny, D.nz, D.nd, D.hx
    seq, x = lax.axis_index("seq"), lax.axis_index("res")
    c = lax.rem(seq, 2)
    d = seq // 2
    y = lax.rem(d, ny)
    z = d // ny
    other = 1 - c

    def dev(z_, y_, c_, x_):
        return ((z_ * ny + y_) * 2 + c_, x_)

    def dev_d(p):
        return dev(p // ny, lax.rem(p, ny), c, x)

    sibling = dev(z, y, other, x)

    def remote(src, dst, ss, rs, to):
        return pltpu.make_async_remote_copy(
            src_ref=src, dst_ref=dst, send_sem=ss, recv_sem=rs, device_id=to, device_id_type=MESH
        )

    def loop(lo, hi, body):
        def step(k, carry):
            body(k)
            return carry

        lax.fori_loop(lo, hi, step, 0)

    def drain(ref, *sems):
        for sem in sems:
            pltpu.make_async_copy(ref, ref, sem).wait()

    def block(i, n):
        return pl.ds(pl.multiple_of(i * n, n), n)

    def turn(i, n):
        j = n - 1 - i
        far = (j + 1) // 2
        return lax.rem(far + (n - 2 * far) * lax.rem(j + 1, 2), n)

    weights = (wk, wv, wq, cq, ck, cv, co)
    wo_copies = [pltpu.make_async_copy(wo.at[:, h], wo_buf.at[h], wo_sem.at[h]) for h in range(hx)]
    w_copies = [pltpu.make_async_copy(w, w_buf.at[n], w_sem.at[n]) for n, w in enumerate(weights)]
    a_in = pltpu.make_async_copy(a_hbm, a_ref, out_sem.at[D.parts])
    a_in.start()
    for n in (0, 2):
        w_copies[n].start()

    bar = pltpu.get_barrier_semaphore()

    def greet(to):
        pl.semaphore_signal(bar, inc=1, device_id=to, device_id_type=MESH)

    def x_core(k):
        xo = lax.rem(x + turn((k - 1) // 2, nx), nx)
        side = lax.rem(k - 1, 2) + jnp.where(k == 2 * nx - 1, 1, 0)
        return xo, lax.rem(c + side, 2)

    def greet_x(k):
        xo, co_ = x_core(k)
        greet(dev(z, y, co_, xo))

    loop(1, 2 * nx, greet_x)
    loop(1, ny, lambda k: greet(dev(z, lax.rem(y + k, ny), c, x)))
    loop(1, nz, lambda k: greet(dev(lax.rem(z + k, nz), y, c, x)))

    a_in.wait()
    def norm_rows(s):
        xn[block(s, D.sites), :] = normed(a_ref[s].astype(F32), g1_ref[...].reshape(1, WIDTH))

    loop(0, D.chains, norm_rows)

    def project(m, h):
        w = jnp.concatenate(
            [w_buf[m, :, (g * hx + h) * HEAD : (g * hx + h + 1) * HEAD] for g in range(nx)], axis=-1
        )
        t = jnp.dot(xn[...], w, preferred_element_type=F32).astype(BF)
        for g in range(nx):
            qkv_s[m, h, g] = jnp.concatenate(
                [
                    t[s * D.sites : (s + 1) * D.sites, g * HEAD : (g + 1) * HEAD]
                    for s in range(D.chains)
                ],
                axis=-1,
            )

    my_sites = block(x, D.sites)
    my_part = block(x, D.psites)

    class Cross:
        def __init__(self, m, h, r=None):
            self.sem = m * hx + h if r is None else (2 + r) * hx + h
            if r is None:
                self.dst = kv_r.at[m, h, my_sites, :]
                self.size = kv_r.at[m, h, pl.ds(0, (nx - 1) * D.sites), :]
                self.src = lambda g: qkv_s.at[m, h, g]
            else:
                self.dst = q_r.at[r, h, my_part, :]
                self.size = q_r.at[r, h, pl.ds(0, (nx - 1) * D.psites), :]
                self.src = lambda g: qkv_s.at[2, h, g, pl.ds(r * D.psites, D.psites), :]

        def copy(self, k):
            xo = lax.rem(x + turn(k - 1, nx), nx)
            return remote(
                self.src(xo), self.dst, x_ss.at[self.sem], x_rs.at[self.sem], dev(z, y, c, xo)
            )

        def keep(self):
            return pltpu.make_async_copy(self.src(x), self.dst, x_ls.at[self.sem])

        def start(self):
            loop(1, nx, lambda k: self.copy(k).start())
            self.keep().start()

        def wait(self):
            self.keep().wait()
            drain(self.size, x_ss.at[self.sem], x_rs.at[self.sem])

    scale = 1.0 / (math.sqrt(HEAD) * math.sqrt(D.total_seqs))
    own_half, far_half = block(c, D.half), block(other, D.half)

    def c_copy(r, h):
        return remote(l_send.at[r, h], l_recv.at[r, h], c_ss.at[r, h], c_rs.at[r, h], sibling)

    def logits(r, h):
        if r == 0:
            Cross(0, h).wait()
        Cross(2, h, r).wait()
        far = lax.dot_general(q_r[r, h, far_half, :], kv_r[0, h], NT, preferred_element_type=F32)
        l_send[r, h] = (far * scale).astype(BF)
        c_copy(r, h).start()
        own = lax.dot_general(q_r[r, h, own_half, :], kv_r[0, h], NT, preferred_element_type=F32)
        l_own[r, h] = own * scale

    def y_copy(r, h, k):
        yo = lax.rem(y + turn(k - 1, ny), ny)
        return remote(
            y_send.at[r, h, block(yo, D.yrows), :],
            y_recv.at[r, h, y],
            y_ss.at[r, h],
            y_rs.at[r, h],
            dev(z, yo, c, x),
        )

    def core_sum(r, h):
        c_copy(r, h).wait()
        total = l_own[r, h] + l_recv[r, h].astype(F32)
        l_own[r, h] = total
        y_send[r, h] = total.astype(BF)
        loop(1, ny, lambda k: y_copy(r, h, k).start())

    zr, slabs = D.zrows, D.total_sites // LANES
    zt = zr * slabs

    def fold(rows):
        n = rows.shape[0] // zr
        return jnp.concatenate(
            [
                rows[i * zr : (i + 1) * zr, j * LANES : (j + 1) * LANES]
                for i in range(n)
                for j in range(slabs)
            ],
            axis=0,
        )

    def unfold(tiles):
        n = tiles.shape[0] // zt
        return jnp.concatenate(
            [
                jnp.concatenate(
                    [tiles[i * zt + j * zr : i * zt + (j + 1) * zr] for i in range(n)], axis=0
                )
                for j in range(slabs)
            ],
            axis=1,
        )

    z_size = pl.ds(0, (nz - 1) * zt)

    def z_copy(r, h, k):
        zo = lax.rem(z + turn(k - 1, nz), nz)
        return remote(
            z_send.at[r, h, block(zo, zt), :],
            z_recv.at[r, h, block(z, zt), :],
            z_ss.at[r, h],
            z_rs.at[r, h],
            dev(zo, y, c, x),
        )

    def y_sum(r, h):
        drain(y_recv.at[r, h, pl.ds(0, ny - 1)], y_ss.at[r, h], y_rs.at[r, h])
        total = l_own[r, h, block(y, D.yrows), :]
        for k in range(1, ny):
            total += y_recv[r, h, lax.rem(y + k, ny)].astype(F32)
        z_send[r, h] = fold(total).astype(BF)
        loop(1, nz, lambda k: z_copy(r, h, k).start())

    def pz_copy(r, h, k):
        zo = lax.rem(z + turn(k - 1, nz), nz)
        return remote(
            p_send.at[r, h], p_z.at[r, h, block(z, zt), :], pz_ss.at[r, h], pz_rs.at[r, h], dev(zo, y, c, x)
        )

    def z_softmax(r, h):
        drain(z_recv.at[r, h, z_size, :], z_ss.at[r, h], z_rs.at[r, h])
        tied = z_send[r, h, block(z, zt), :].astype(F32)
        for k in range(1, nz):
            tied += z_recv[r, h, block(lax.rem(z + k, nz), zt), :].astype(F32)
        prob = fold(softmax(unfold(tied))).astype(BF)
        p_send[r, h] = prob
        loop(1, nz, lambda k: pz_copy(r, h, k).start())
        p_z[r, h, block(z, zt), :] = prob

    py_rows = block(c * ny + y, D.yrows)

    def py_copy(r, h, k):
        yo = lax.rem(y + turn(k - 1, ny), ny)
        place = p_full.at[r, h, py_rows, :]
        return remote(place, place, py_ss.at[r, h], py_rs.at[r, h], dev(z, yo, c, x))

    def gather_z(r, h):
        drain(p_z.at[r, h, z_size, :], pz_ss.at[r, h], pz_rs.at[r, h])
        p_full[r, h, py_rows, :] = unfold(p_z[r, h].astype(F32)).astype(BF)
        loop(1, ny, lambda k: py_copy(r, h, k).start())

    def pc_copy(r, h):
        place = p_full.at[r, h, own_half, :]
        return remote(place, place, pc_ss.at[r, h], pc_rs.at[r, h], sibling)

    def gather_y(r, h):
        drain(p_full.at[r, h, pl.ds(0, (ny - 1) * D.yrows), :], py_ss.at[r, h], py_rs.at[r, h])
        pc_copy(r, h).start()

    def o_rows(xo, core):
        return block(xo * 2 + core, D.csites)

    def o_copy(r, h, k):
        xo, co_ = x_core(k)
        return remote(
            o_send.at[r, h, o_rows(xo, co_), :],
            m_recv.at[r, c, h, x],
            o_ss.at[r, h],
            o_rs.at[r, h],
            dev(z, y, co_, xo),
        )

    def o_local(r, h):
        return pltpu.make_async_copy(
            o_send.at[r, h, o_rows(x, c), :], m_recv.at[r, c, h, x], o_ls.at[r, h]
        )

    def attend(r, h):
        if r == 0:
            Cross(1, h).wait()
        pc_copy(r, h).wait()
        o_send[r, h] = jnp.dot(p_full[r, h], kv_r[1, h], preferred_element_type=F32).astype(BF)
        loop(1, 2 * nx, lambda k: o_copy(r, h, k).start())
        o_local(r, h).start()

    def pack(slabs):
        pieces = [v.reshape(nd, D.pair, LANES) for v in slabs]
        left = jnp.concatenate(pieces[: SLABS // 2], axis=-1)
        right = jnp.concatenate(pieces[SLABS // 2 :], axis=-1)
        return jnp.concatenate([left, right], axis=1).astype(BF).reshape(2 * D.col_len, WIDTH // 2)

    def unpack(packed):
        t = packed.reshape(nd, 2 * D.pair, WIDTH // 2).astype(F32)
        both = jnp.concatenate([t[:, : D.pair], t[:, D.pair :]], axis=-1)
        return both.reshape(D.col_len, WIDTH)

    def d_copies(r, src, dst, ss, rs, ls):
        def copy(k):
            j = nz - 1 - (k - 1) // ny
            dz = turn((k - 1) // ny, nz)
            dy = lax.rem(k - 1, ny) + jnp.where(j == 0, 1, 0)
            p = lax.rem(z + dz, nz) * ny + lax.rem(y + dy, ny)
            return remote(
                src.at[r, block(p, 2 * D.pair), :], dst.at[r, block(d, 2 * D.pair), :], ss.at[r], rs.at[r], dev_d(p)
            )

        mine = block(d, 2 * D.pair)
        keep = pltpu.make_async_copy(src.at[r, mine, :], dst.at[r, mine, :], ls.at[r])
        return copy, keep

    def d_start(r, *refs):
        copy, keep = d_copies(r, *refs)
        loop(1, nd, lambda k: copy(k).start())
        keep.start()

    def d_wait(r, src, dst, ss, rs, ls):
        d_copies(r, src, dst, ss, rs, ls)[1].wait()
        drain(dst.at[r, pl.ds(0, (nd - 1) * 2 * D.pair), :], ss.at[r], rs.at[r])

    into = (c_send, c_recv, i_ss, i_rs, i_ls)
    back = (r_send, r_recv, b_ss, b_rs, b_ls)

    def a_rows(r, core):
        return block(r * 2 + core, D.csites)

    def residual_copies():
        copies = []
        for r in range(D.parts):
            keep = pltpu.make_async_copy(a_ref.at[:, a_rows(r, c), :], a_res.at[r, c], a_ls.at[r])
            swap = remote(a_ref.at[:, a_rows(r, other), :], a_res.at[r, c], a_ss.at[r], a_rs.at[r], sibling)
            keep.start()
            swap.start()
            copies.append((keep, swap))
        return copies

    def mixing(r, h):
        o_local(r, h).wait()
        drain(o_send.at[r, h, pl.ds(0, (2 * nx - 1) * D.csites), :], o_ss.at[r, h], o_rs.at[r, h])
        chains = [(cc, s) for cc in range(2) for s in range(D.chains)]
        for n, (cc, s) in enumerate(chains):
            mix[n * D.csites : (n + 1) * D.csites, :] = jnp.concatenate(
                [m_recv[r, cc, h, g, :, s * HEAD : (s + 1) * HEAD] for g in range(nx)], axis=-1
            )
        if h == 0:
            for copy in a_copies[r]:
                copy.wait()
            for n, (cc, s) in enumerate(chains):
                acc[r, n * D.csites : (n + 1) * D.csites, :] = a_res[r, cc, s].astype(F32)

        def columns(cb):
            cols = block(cb, 256)
            part = wo_buf[h, :, :, cols].reshape(nx * HEAD, 256)
            total = acc[r, :, cols] + jnp.dot(mix[...], part, preferred_element_type=F32)
            if h < hx - 1:
                acc[r, :, cols] = total
            else:
                for n in range(D.pair):
                    for j in range(2):
                        c_f32[cb * 2 + j, pl.ds(n, D.csites, stride=D.pair), :] = total[
                            n * D.csites : (n + 1) * D.csites, j * LANES : (j + 1) * LANES
                        ]

        loop(0, WIDTH // 256, columns)

    def after_row(r):
        mixing(r, hx - 1)
        c_send[r] = pack([c_f32[j] for j in range(SLABS)])
        d_start(r, *into)

    col_scale = 1.0 / math.sqrt(HEAD)
    lane = lax.broadcasted_iota(jnp.int32, (1, 2 * HEAD), 1)

    def column(r):
        d_wait(r, *into)
        wide = unpack(c_recv[r])
        wide_buf[...] = wide
        cn[...] = normed(wide, g2_ref[...].reshape(1, WIDTH))
        for m in range(3):
            c_qkv[m] = jnp.dot(cn[...], w_buf[3 + m], preferred_element_type=F32).astype(BF)

        def two_heads(p):
            cols = block(p, 2 * HEAD)
            q, k, v = c_qkv[0, :, cols], c_qkv[1, :, cols], c_qkv[2, :, cols]
            zero = jnp.zeros_like(k)
            mixed = None
            for side in range(2):
                mine = (lane < HEAD) if side == 0 else (lane >= HEAD)
                scores = lax.dot_general(
                    q, jnp.where(mine, k, zero), NT, preferred_element_type=F32
                )
                prob = softmax(scores * col_scale).astype(BF)
                part = jnp.dot(prob, jnp.where(mine, v, zero), preferred_element_type=F32)
                mixed = part if mixed is None else mixed + part
            c_mix[:, cols] = mixed.astype(BF)

        loop(0, HEADS // 2, two_heads)
        change = jnp.dot(c_mix[...], w_buf[6], preferred_element_type=F32)
        total = wide_buf[...] + change
        r_send[r] = pack([total[:, j * LANES : (j + 1) * LANES] for j in range(SLABS)])
        d_start(r, *back)

    def f_copy(r):
        return remote(f_send.at[r], out_ref.at[:, a_rows(r, c), :], f_ss.at[r], f_rs.at[r], sibling)

    def out_copy(r):
        return pltpu.make_async_copy(out_v.at[r], out_ref.at[:, a_rows(r, c), :], out_sem.at[r])

    def finish(r):
        d_wait(r, *back)
        total = unpack(r_recv[r])
        for j in range(SLABS):
            c_f32[j] = total[:, j * LANES : (j + 1) * LANES]

        def chain_rows(s):
            rows = pl.ds(s, D.csites, stride=D.pair)
            return jnp.concatenate([c_f32[j, rows, :] for j in range(SLABS)], axis=1).astype(BF)

        for s in range(D.chains):
            f_send[r, s] = chain_rows(other * D.chains + s)
        f_copy(r).start()
        for s in range(D.chains):
            out_v[r, s] = chain_rows(c * D.chains + s)
        out_copy(r).start()

    for m in (0, 2):
        w_copies[m].wait()
    for n in (1, 3, 4, 5, 6):
        w_copies[n].start()
    for copy in wo_copies:
        copy.start()

    def first(h):
        Cross(0, h).start()
        Cross(2, h, 0).start()

    project(0, 0)
    project(2, 0)
    pl.semaphore_wait(bar, 2 * nx - 1 + ny - 1 + nz - 1)
    first(0)
    project(0, 1)
    project(2, 1)
    first(1)
    project(0, 2)
    project(2, 2)
    a_copies = residual_copies()
    w_copies[1].wait()
    for h in range(hx):
        project(1, h)

    def queries(h):
        Cross(2, h, 1).start()

    def values(h):
        Cross(1, h).start()

    def weights_in():
        for n in range(3, 7):
            w_copies[n].wait()
        for copy in wo_copies:
            copy.wait()

    plan = (
        (logits, 0, 0), (first, 2), (core_sum, 0, 0), (logits, 0, 1), (queries, 0), (queries, 1), (queries, 2),
        (core_sum, 0, 1), (y_sum, 0, 0), (logits, 0, 2), (values, 0), (values, 1), (values, 2),
        (core_sum, 0, 2), (y_sum, 0, 1), (logits, 1, 0), (z_softmax, 0, 0), (core_sum, 1, 0), (logits, 1, 1),
        (core_sum, 1, 1), (logits, 1, 2), (core_sum, 1, 2), (y_sum, 0, 2), (z_softmax, 0, 1), (gather_z, 0, 0),
        (y_sum, 1, 0), (y_sum, 1, 1), (y_sum, 1, 2), (z_softmax, 0, 2), (gather_z, 0, 1), (gather_y, 0, 0),
        (z_softmax, 1, 0), (attend, 0, 0), (z_softmax, 1, 1), (z_softmax, 1, 2), (gather_z, 0, 2),
        (gather_y, 0, 1), (attend, 0, 1), (gather_z, 1, 0), (gather_z, 1, 1), (weights_in,), (mixing, 0, 0),
        (gather_z, 1, 2), (gather_y, 0, 2), (attend, 0, 2), (gather_y, 1, 0), (attend, 1, 0), (mixing, 0, 1),
        (gather_y, 1, 1), (attend, 1, 1), (after_row, 0), (gather_y, 1, 2), (attend, 1, 2), (mixing, 1, 0),
        (mixing, 1, 1), (after_row, 1), (column, 0), (column, 1), (finish, 0), (finish, 1),
    )
    for step, *args in plan:
        step(*args)
    for r in range(D.parts):
        f_copy(r).wait()
        out_copy(r).wait()


def on_device(D, a, g1, wq, wk, wv, wo, g2, cq, ck, cv, co):
    vmem = pl.BlockSpec(memory_space=pltpu.VMEM)
    hbm = pl.BlockSpec(memory_space=pl.ANY)
    sites, N, H, L = D.total_sites, D.parts, D.hx, D.chains * HEAD
    bf = lambda *shape: pltpu.VMEM(shape, BF)
    f32 = lambda *shape: pltpu.VMEM(shape, F32)
    sem = lambda *shape: pltpu.SemaphoreType.DMA(shape)
    scratch = dict(
        a_ref=bf(D.chains, D.sites, WIDTH),
        out_v=bf(N, D.chains, D.csites, WIDTH),
        w_buf=bf(7, WIDTH, WIDTH),
        xn=bf(D.rows, WIDTH),
        qkv_s=bf(3, D.hx, D.nx, D.sites, L),
        kv_r=bf(2, H, sites, L),
        q_r=bf(N, H, D.prows, L),
        l_own=f32(N, H, D.half, sites),
        l_send=bf(N, H, D.half, sites),
        l_recv=bf(N, H, D.half, sites),
        y_send=bf(N, H, D.half, sites),
        y_recv=bf(N, H, D.ny, D.yrows, sites),
        z_send=bf(N, H, D.yrows * sites // LANES, LANES),
        z_recv=bf(N, H, D.yrows * sites // LANES, LANES),
        p_send=bf(N, H, D.zrows * sites // LANES, LANES),
        p_z=bf(N, H, D.yrows * sites // LANES, LANES),
        p_full=bf(N, H, D.prows, sites),
        o_send=bf(N, H, D.prows, L),
        m_recv=bf(N, 2, H, D.nx, D.csites, L),
        wo_buf=bf(H, D.nx, HEAD, WIDTH),
        acc=f32(N, D.col_len, WIDTH),
        a_res=bf(N, 2, D.chains, D.csites, WIDTH),
        mix=bf(D.pair * D.csites, L),
        c_f32=f32(SLABS, D.col_len, LANES),
        c_send=bf(N, 2 * D.col_len, WIDTH // 2),
        c_recv=bf(N, 2 * D.col_len, WIDTH // 2),
        wide_buf=f32(D.col_len, WIDTH),
        cn=bf(D.col_len, WIDTH),
        c_qkv=bf(3, D.col_len, WIDTH),
        c_mix=bf(D.col_len, WIDTH),
        r_send=bf(N, 2 * D.col_len, WIDTH // 2),
        r_recv=bf(N, 2 * D.col_len, WIDTH // 2),
        f_send=bf(N, D.chains, D.csites, WIDTH),
        w_sem=sem(7), wo_sem=sem(H),
        x_ss=sem((2 + N) * H), x_rs=sem((2 + N) * H), x_ls=sem((2 + N) * H),
        a_ls=sem(N), a_ss=sem(N), a_rs=sem(N),
        c_ss=sem(N, H), c_rs=sem(N, H), y_ss=sem(N, H), y_rs=sem(N, H), z_ss=sem(N, H), z_rs=sem(N, H),
        pz_ss=sem(N, H), pz_rs=sem(N, H), py_ss=sem(N, H), py_rs=sem(N, H), pc_ss=sem(N, H), pc_rs=sem(N, H),
        o_ss=sem(N, H), o_rs=sem(N, H), o_ls=sem(N, H),
        i_ss=sem(N), i_rs=sem(N), i_ls=sem(N), b_ss=sem(N), b_rs=sem(N), b_ls=sem(N),
        f_ss=sem(N), f_rs=sem(N), out_sem=sem(N + 1),
    )
    flops = 2 * (8 * D.rows * WIDTH * WIDTH + 2 * D.hx * sites * sites * L)
    return pl.pallas_call(
        functools.partial(layer, D),
        out_shape=jax.ShapeDtypeStruct(a.shape, a.dtype),
        in_specs=[hbm] + [vmem] * 2 + [hbm] * 8,
        out_specs=hbm,
        scratch_shapes=list(scratch.values()),
        compiler_params=pltpu.CompilerParams(
            collective_id=0, has_side_effects=True, vmem_limit_bytes=60 * 2**20
        ),
        cost_estimate=pl.CostEstimate(flops=flops, bytes_accessed=12 * 2**20, transcendentals=2**21),
        name="msa_layer",
    )(a, g1, g2, wq, wk, wv, wo.reshape(D.nx, H, HEAD, WIDTH), cq, ck, cv, co)


def solution(mesh):
    nseq, nx = mesh.shape["seq"], mesh.shape["res"]
    ny = 4

    def step(a, *rest):
        D = Dims(nseq, nx, ny, a.shape[0], a.shape[1])
        return on_device(D, a, *rest)

    in_specs = (P("seq", "res", None),) + (P(),) * 10
    return jax.shard_map(
        step, mesh=mesh, in_specs=in_specs, out_specs=P("seq", "res", None), check_vma=False
    )
```

```python
import functools
import math

import jax
import jax.numpy as jnp
from jax import lax
from jax.experimental import pallas as pl
from jax.experimental.pallas import tpu as pltpu
from jax.sharding import PartitionSpec as P

MESH = pl.DeviceIdType.MESH
HEADS = 12
HEAD = 64
WIDTH = HEADS * HEAD
LANES = 128
SLABS = WIDTH // LANES
BF = jnp.bfloat16
F32 = jnp.float32
NT = (((1,), (1,)), ((), ()))


class Dims:
    def __init__(self, nseq, nx, ny, chains, sites):
        self.nx, self.ny = nx, ny
        self.nz = nseq // (2 * ny)
        self.nd = self.ny * self.nz
        self.chains, self.sites = chains, sites
        self.rows = chains * sites
        self.hx = HEADS // nx
        self.total_sites = sites * nx
        self.parts = sites // (2 * self.nd)
        self.psites = sites // self.parts
        self.csites = self.psites // 2
        self.prows = self.psites * nx
        self.half = self.prows // 2
        self.yrows = self.half // ny
        self.zrows = self.yrows // self.nz
        self.pair = 2 * chains
        self.col_len = self.nd * self.pair
        self.total_seqs = nseq * chains
        assert self.csites == self.nd and self.pair == 8 and self.zrows == 4


def normed(wide, gain):
    center = wide - jnp.mean(wide, axis=-1, keepdims=True)
    spread = jnp.mean(center * center, axis=-1, keepdims=True)
    return (center * lax.rsqrt(spread + 1e-05) * gain).astype(BF)


def softmax(scores):
    top = jnp.max(scores, axis=-1, keepdims=True)
    e = jnp.exp(scores - top)
    return e / jnp.sum(e, axis=-1, keepdims=True)


def layer(
    D,
    a_hbm, g1_ref, g2_ref,
    wq, wk, wv, wo, cq, ck, cv, co,
    out_ref,
    a_ref, out_v, w_buf, xn, qkv_s, kv_r, q_r, l_own, l_send, l_recv, y_send, y_recv, z_send, z_recv,
    p_send, p_z, p_full, o_send, m_recv, wo_buf, acc, a_res, mix, c_f32, c_send, c_recv, wide_buf, cn, c_qkv, c_mix,
    r_send, r_recv, f_send,
    w_sem, wo_sem, x_ss, x_rs, x_ls, a_ls, a_ss, a_rs, c_ss, c_rs, y_ss, y_rs, z_ss, z_rs, pz_ss, pz_rs, py_ss, py_rs,
    pc_ss, pc_rs, o_ss, o_rs, o_ls, i_ss, i_rs, i_ls, b_ss, b_rs, b_ls, f_ss, f_rs, out_sem,
):
    nx, ny, nz, nd, hx = D.nx, D.ny, D.nz, D.nd, D.hx
    seq, x = lax.axis_index("seq"), lax.axis_index("res")
    c = lax.rem(seq, 2)
    d = seq // 2
    y = lax.rem(d, ny)
    z = d // ny
    other = 1 - c

    def dev(z_, y_, c_, x_):
        return ((z_ * ny + y_) * 2 + c_, x_)

    def dev_d(p):
        return dev(p // ny, lax.rem(p, ny), c, x)

    sibling = dev(z, y, other, x)

    def remote(src, dst, ss, rs, to):
        return pltpu.make_async_remote_copy(
            src_ref=src, dst_ref=dst, send_sem=ss, recv_sem=rs, device_id=to, device_id_type=MESH
        )

    def loop(lo, hi, body):
        def step(k, carry):
            body(k)
            return carry

        lax.fori_loop(lo, hi, step, 0)

    def drain(ref, *sems):
        for sem in sems:
            pltpu.make_async_copy(ref, ref, sem).wait()

    def block(i, n):
        return pl.ds(pl.multiple_of(i * n, n), n)

    def turn(i, n):
        j = n - 1 - i
        far = (j + 1) // 2
        return lax.rem(far + (n - 2 * far) * lax.rem(j + 1, 2), n)

    weights = (wk, wv, wq, cq, ck, cv, co)
    wo_copies = [pltpu.make_async_copy(wo.at[:, h], wo_buf.at[h], wo_sem.at[h]) for h in range(hx)]
    w_copies = [pltpu.make_async_copy(w, w_buf.at[n], w_sem.at[n]) for n, w in enumerate(weights)]
    a_in = pltpu.make_async_copy(a_hbm, a_ref, out_sem.at[D.parts])
    a_in.start()
    for n in (0, 2):
        w_copies[n].start()

    bar = pltpu.get_barrier_semaphore()

    def greet(to):
        pl.semaphore_signal(bar, inc=1, device_id=to, device_id_type=MESH)

    def x_core(k):
        xo = lax.rem(x + turn((k - 1) // 2, nx), nx)
        side = lax.rem(k - 1, 2) + jnp.where(k == 2 * nx - 1, 1, 0)
        return xo, lax.rem(c + side, 2)

    def greet_x(k):
        xo, co_ = x_core(k)
        greet(dev(z, y, co_, xo))

    loop(1, 2 * nx, greet_x)
    loop(1, ny, lambda k: greet(dev(z, lax.rem(y + k, ny), c, x)))
    loop(1, nz, lambda k: greet(dev(lax.rem(z + k, nz), y, c, x)))

    a_in.wait()
    def norm_rows(s):
        xn[block(s, D.sites), :] = normed(a_ref[s].astype(F32), g1_ref[...].reshape(1, WIDTH))

    loop(0, D.chains, norm_rows)

    def project(m, h):
        w = jnp.concatenate(
            [w_buf[m, :, (g * hx + h) * HEAD : (g * hx + h + 1) * HEAD] for g in range(nx)], axis=-1
        )
        t = jnp.dot(xn[...], w, preferred_element_type=F32).astype(BF)
        for g in range(nx):
            qkv_s[m, h, g] = jnp.concatenate(
                [
                    t[s * D.sites : (s + 1) * D.sites, g * HEAD : (g + 1) * HEAD]
                    for s in range(D.chains)
                ],
                axis=-1,
            )

    my_sites = block(x, D.sites)
    my_part = block(x, D.psites)

    class Cross:
        def __init__(self, m, h, r=None):
            self.sem = m * hx + h if r is None else (2 + r) * hx + h
            if r is None:
                self.dst = kv_r.at[m, h, my_sites, :]
                self.size = kv_r.at[m, h, pl.ds(0, (nx - 1) * D.sites), :]
                self.src = lambda g: qkv_s.at[m, h, g]
            else:
                self.dst = q_r.at[r, h, my_part, :]
                self.size = q_r.at[r, h, pl.ds(0, (nx - 1) * D.psites), :]
                self.src = lambda g: qkv_s.at[2, h, g, pl.ds(r * D.psites, D.psites), :]

        def copy(self, k):
            xo = lax.rem(x + turn(k - 1, nx), nx)
            return remote(
                self.src(xo), self.dst, x_ss.at[self.sem], x_rs.at[self.sem], dev(z, y, c, xo)
            )

        def keep(self):
            return pltpu.make_async_copy(self.src(x), self.dst, x_ls.at[self.sem])

        def start(self):
            loop(1, nx, lambda k: self.copy(k).start())
            self.keep().start()

        def wait(self):
            self.keep().wait()
            drain(self.size, x_ss.at[self.sem], x_rs.at[self.sem])

    scale = 1.0 / (math.sqrt(HEAD) * math.sqrt(D.total_seqs))
    own_half, far_half = block(c, D.half), block(other, D.half)

    def c_copy(r, h):
        return remote(l_send.at[r, h], l_recv.at[r, h], c_ss.at[r, h], c_rs.at[r, h], sibling)

    def logits(r, h):
        if r == 0:
            Cross(0, h).wait()
        Cross(2, h, r).wait()
        far = lax.dot_general(q_r[r, h, far_half, :], kv_r[0, h], NT, preferred_element_type=F32)
        l_send[r, h] = (far * scale).astype(BF)
        c_copy(r, h).start()
        own = lax.dot_general(q_r[r, h, own_half, :], kv_r[0, h], NT, preferred_element_type=F32)
        l_own[r, h] = own * scale

    def y_copy(r, h, k):
        yo = lax.rem(y + turn(k - 1, ny), ny)
        return remote(
            y_send.at[r, h, block(yo, D.yrows), :],
            y_recv.at[r, h, y],
            y_ss.at[r, h],
            y_rs.at[r, h],
            dev(z, yo, c, x),
        )

    def core_sum(r, h):
        c_copy(r, h).wait()
        total = l_own[r, h] + l_recv[r, h].astype(F32)
        l_own[r, h] = total
        y_send[r, h] = total.astype(BF)
        loop(1, ny, lambda k: y_copy(r, h, k).start())

    zr, slabs = D.zrows, D.total_sites // LANES
    zt = zr * slabs

    def fold(rows):
        n = rows.shape[0] // zr
        return jnp.concatenate(
            [
                rows[i * zr : (i + 1) * zr, j * LANES : (j + 1) * LANES]
                for i in range(n)
                for j in range(slabs)
            ],
            axis=0,
        )

    def unfold(tiles):
        n = tiles.shape[0] // zt
        return jnp.concatenate(
            [
                jnp.concatenate(
                    [tiles[i * zt + j * zr : i * zt + (j + 1) * zr] for i in range(n)], axis=0
                )
                for j in range(slabs)
            ],
            axis=1,
        )

    z_size = pl.ds(0, (nz - 1) * zt)

    def z_copy(r, h, k):
        zo = lax.rem(z + turn(k - 1, nz), nz)
        return remote(
            z_send.at[r, h, block(zo, zt), :],
            z_recv.at[r, h, block(z, zt), :],
            z_ss.at[r, h],
            z_rs.at[r, h],
            dev(zo, y, c, x),
        )

    def y_sum(r, h):
        drain(y_recv.at[r, h, pl.ds(0, ny - 1)], y_ss.at[r, h], y_rs.at[r, h])
        total = l_own[r, h, block(y, D.yrows), :]
        for k in range(1, ny):
            total += y_recv[r, h, lax.rem(y + k, ny)].astype(F32)
        z_send[r, h] = fold(total).astype(BF)
        loop(1, nz, lambda k: z_copy(r, h, k).start())

    def pz_copy(r, h, k):
        zo = lax.rem(z + turn(k - 1, nz), nz)
        return remote(
            p_send.at[r, h], p_z.at[r, h, block(z, zt), :], pz_ss.at[r, h], pz_rs.at[r, h], dev(zo, y, c, x)
        )

    def z_softmax(r, h):
        drain(z_recv.at[r, h, z_size, :], z_ss.at[r, h], z_rs.at[r, h])
        tied = z_send[r, h, block(z, zt), :].astype(F32)
        for k in range(1, nz):
            tied += z_recv[r, h, block(lax.rem(z + k, nz), zt), :].astype(F32)
        prob = fold(softmax(unfold(tied))).astype(BF)
        p_send[r, h] = prob
        loop(1, nz, lambda k: pz_copy(r, h, k).start())
        p_z[r, h, block(z, zt), :] = prob

    py_rows = block(c * ny + y, D.yrows)

    def py_copy(r, h, k):
        yo = lax.rem(y + turn(k - 1, ny), ny)
        place = p_full.at[r, h, py_rows, :]
        return remote(place, place, py_ss.at[r, h], py_rs.at[r, h], dev(z, yo, c, x))

    def gather_z(r, h):
        drain(p_z.at[r, h, z_size, :], pz_ss.at[r, h], pz_rs.at[r, h])
        p_full[r, h, py_rows, :] = unfold(p_z[r, h].astype(F32)).astype(BF)
        loop(1, ny, lambda k: py_copy(r, h, k).start())

    def pc_copy(r, h):
        place = p_full.at[r, h, own_half, :]
        return remote(place, place, pc_ss.at[r, h], pc_rs.at[r, h], sibling)

    def gather_y(r, h):
        drain(p_full.at[r, h, pl.ds(0, (ny - 1) * D.yrows), :], py_ss.at[r, h], py_rs.at[r, h])
        pc_copy(r, h).start()

    def o_rows(xo, core):
        return block(xo * 2 + core, D.csites)

    def o_copy(r, h, k):
        xo, co_ = x_core(k)
        return remote(
            o_send.at[r, h, o_rows(xo, co_), :],
            m_recv.at[r, c, h, x],
            o_ss.at[r, h],
            o_rs.at[r, h],
            dev(z, y, co_, xo),
        )

    def o_local(r, h):
        return pltpu.make_async_copy(
            o_send.at[r, h, o_rows(x, c), :], m_recv.at[r, c, h, x], o_ls.at[r, h]
        )

    def attend(r, h):
        if r == 0:
            Cross(1, h).wait()
        pc_copy(r, h).wait()
        o_send[r, h] = jnp.dot(p_full[r, h], kv_r[1, h], preferred_element_type=F32).astype(BF)
        loop(1, 2 * nx, lambda k: o_copy(r, h, k).start())
        o_local(r, h).start()

    def pack(slabs):
        pieces = [v.reshape(nd, D.pair, LANES) for v in slabs]
        left = jnp.concatenate(pieces[: SLABS // 2], axis=-1)
        right = jnp.concatenate(pieces[SLABS // 2 :], axis=-1)
        return jnp.concatenate([left, right], axis=1).astype(BF).reshape(2 * D.col_len, WIDTH // 2)

    def unpack(packed):
        t = packed.reshape(nd, 2 * D.pair, WIDTH // 2).astype(F32)
        both = jnp.concatenate([t[:, : D.pair], t[:, D.pair :]], axis=-1)
        return both.reshape(D.col_len, WIDTH)

    def d_copies(r, src, dst, ss, rs, ls):
        def copy(k):
            j = nz - 1 - (k - 1) // ny
            dz = turn((k - 1) // ny, nz)
            dy = lax.rem(k - 1, ny) + jnp.where(j == 0, 1, 0)
            p = lax.rem(z + dz, nz) * ny + lax.rem(y + dy, ny)
            return remote(
                src.at[r, block(p, 2 * D.pair), :], dst.at[r, block(d, 2 * D.pair), :], ss.at[r], rs.at[r], dev_d(p)
            )

        mine = block(d, 2 * D.pair)
        keep = pltpu.make_async_copy(src.at[r, mine, :], dst.at[r, mine, :], ls.at[r])
        return copy, keep

    def d_start(r, *refs):
        copy, keep = d_copies(r, *refs)
        loop(1, nd, lambda k: copy(k).start())
        keep.start()

    def d_wait(r, src, dst, ss, rs, ls):
        d_copies(r, src, dst, ss, rs, ls)[1].wait()
        drain(dst.at[r, pl.ds(0, (nd - 1) * 2 * D.pair), :], ss.at[r], rs.at[r])

    into = (c_send, c_recv, i_ss, i_rs, i_ls)
    back = (r_send, r_recv, b_ss, b_rs, b_ls)

    def a_rows(r, core):
        return block(r * 2 + core, D.csites)

    def residual_copies():
        copies = []
        for r in range(D.parts):
            keep = pltpu.make_async_copy(a_ref.at[:, a_rows(r, c), :], a_res.at[r, c], a_ls.at[r])
            swap = remote(a_ref.at[:, a_rows(r, other), :], a_res.at[r, c], a_ss.at[r], a_rs.at[r], sibling)
            keep.start()
            swap.start()
            copies.append((keep, swap))
        return copies

    def mixing(r, h):
        o_local(r, h).wait()
        drain(o_send.at[r, h, pl.ds(0, (2 * nx - 1) * D.csites), :], o_ss.at[r, h], o_rs.at[r, h])
        chains = [(cc, s) for cc in range(2) for s in range(D.chains)]
        for n, (cc, s) in enumerate(chains):
            mix[n * D.csites : (n + 1) * D.csites, :] = jnp.concatenate(
                [m_recv[r, cc, h, g, :, s * HEAD : (s + 1) * HEAD] for g in range(nx)], axis=-1
            )
        if h == 0:
            for copy in a_copies[r]:
                copy.wait()
            for n, (cc, s) in enumerate(chains):
                acc[r, n * D.csites : (n + 1) * D.csites, :] = a_res[r, cc, s].astype(F32)

        def columns(cb):
            cols = block(cb, 256)
            part = wo_buf[h, :, :, cols].reshape(nx * HEAD, 256)
            total = acc[r, :, cols] + jnp.dot(mix[...], part, preferred_element_type=F32)
            if h < hx - 1:
                acc[r, :, cols] = total
            else:
                for n in range(D.pair):
                    for j in range(2):
                        c_f32[cb * 2 + j, pl.ds(n, D.csites, stride=D.pair), :] = total[
                            n * D.csites : (n + 1) * D.csites, j * LANES : (j + 1) * LANES
                        ]

        loop(0, WIDTH // 256, columns)

    def after_row(r):
        mixing(r, hx - 1)
        c_send[r] = pack([c_f32[j] for j in range(SLABS)])
        d_start(r, *into)

    col_scale = 1.0 / math.sqrt(HEAD)
    lane = lax.broadcasted_iota(jnp.int32, (1, 2 * HEAD), 1)

    def column(r):
        d_wait(r, *into)
        wide = unpack(c_recv[r])
        wide_buf[...] = wide
        cn[...] = normed(wide, g2_ref[...].reshape(1, WIDTH))
        for m in range(3):
            c_qkv[m] = jnp.dot(cn[...], w_buf[3 + m], preferred_element_type=F32).astype(BF)

        def two_heads(p):
            cols = block(p, 2 * HEAD)
            q, k, v = c_qkv[0, :, cols], c_qkv[1, :, cols], c_qkv[2, :, cols]
            zero = jnp.zeros_like(k)
            mixed = None
            for side in range(2):
                mine = (lane < HEAD) if side == 0 else (lane >= HEAD)
                scores = lax.dot_general(
                    q, jnp.where(mine, k, zero), NT, preferred_element_type=F32
                )
                prob = softmax(scores * col_scale).astype(BF)
                part = jnp.dot(prob, jnp.where(mine, v, zero), preferred_element_type=F32)
                mixed = part if mixed is None else mixed + part
            c_mix[:, cols] = mixed.astype(BF)

        loop(0, HEADS // 2, two_heads)
        change = jnp.dot(c_mix[...], w_buf[6], preferred_element_type=F32)
        total = wide_buf[...] + change
        r_send[r] = pack([total[:, j * LANES : (j + 1) * LANES] for j in range(SLABS)])
        d_start(r, *back)

    def f_copy(r):
        return remote(f_send.at[r], out_ref.at[:, a_rows(r, c), :], f_ss.at[r], f_rs.at[r], sibling)

    def out_copy(r):
        return pltpu.make_async_copy(out_v.at[r], out_ref.at[:, a_rows(r, c), :], out_sem.at[r])

    def finish(r):
        d_wait(r, *back)
        total = unpack(r_recv[r])
        for j in range(SLABS):
            c_f32[j] = total[:, j * LANES : (j + 1) * LANES]

        def chain_rows(s):
            rows = pl.ds(s, D.csites, stride=D.pair)
            return jnp.concatenate([c_f32[j, rows, :] for j in range(SLABS)], axis=1).astype(BF)

        for s in range(D.chains):
            f_send[r, s] = chain_rows(other * D.chains + s)
        f_copy(r).start()
        for s in range(D.chains):
            out_v[r, s] = chain_rows(c * D.chains + s)
        out_copy(r).start()

    for m in (0, 2):
        w_copies[m].wait()
    for n in (1, 3, 4, 5, 6):
        w_copies[n].start()
    for copy in wo_copies:
        copy.start()

    def first(h):
        Cross(0, h).start()
        Cross(2, h, 0).start()

    project(0, 0)
    project(2, 0)
    pl.semaphore_wait(bar, 2 * nx - 1 + ny - 1 + nz - 1)
    first(0)
    project(0, 1)
    project(2, 1)
    first(1)
    project(0, 2)
    project(2, 2)
    a_copies = residual_copies()
    w_copies[1].wait()
    for h in range(hx):
        project(1, h)

    def queries(h):
        Cross(2, h, 1).start()

    def values(h):
        Cross(1, h).start()

    def weights_in():
        for n in range(3, 7):
            w_copies[n].wait()
        for copy in wo_copies:
            copy.wait()

    plan = (
        (logits, 0, 0), (first, 2), (core_sum, 0, 0), (logits, 0, 1), (queries, 0), (queries, 1), (queries, 2),
        (core_sum, 0, 1), (y_sum, 0, 0), (logits, 0, 2), (values, 0), (values, 1), (values, 2),
        (core_sum, 0, 2), (y_sum, 0, 1), (logits, 1, 0), (z_softmax, 0, 0), (core_sum, 1, 0), (logits, 1, 1),
        (core_sum, 1, 1), (logits, 1, 2), (core_sum, 1, 2), (y_sum, 0, 2), (z_softmax, 0, 1), (gather_z, 0, 0),
        (y_sum, 1, 0), (y_sum, 1, 1), (y_sum, 1, 2), (z_softmax, 0, 2), (gather_z, 0, 1), (gather_y, 0, 0),
        (z_softmax, 1, 0), (attend, 0, 0), (z_softmax, 1, 1), (z_softmax, 1, 2), (gather_z, 0, 2),
        (gather_y, 0, 1), (attend, 0, 1), (gather_z, 1, 0), (gather_z, 1, 1), (weights_in,), (mixing, 0, 0),
        (gather_z, 1, 2), (gather_y, 0, 2), (attend, 0, 2), (gather_y, 1, 0), (attend, 1, 0), (mixing, 0, 1),
        (gather_y, 1, 1), (attend, 1, 1), (mixing, 1, 0), (after_row, 0), (gather_y, 1, 2), (attend, 1, 2),
        (mixing, 1, 1), (after_row, 1), (column, 0), (column, 1), (finish, 0), (finish, 1),
    )
    for step, *args in plan:
        step(*args)
    for r in range(D.parts):
        f_copy(r).wait()
        out_copy(r).wait()


def on_device(D, a, g1, wq, wk, wv, wo, g2, cq, ck, cv, co):
    vmem = pl.BlockSpec(memory_space=pltpu.VMEM)
    hbm = pl.BlockSpec(memory_space=pl.ANY)
    sites, N, H, L = D.total_sites, D.parts, D.hx, D.chains * HEAD
    bf = lambda *shape: pltpu.VMEM(shape, BF)
    f32 = lambda *shape: pltpu.VMEM(shape, F32)
    sem = lambda *shape: pltpu.SemaphoreType.DMA(shape)
    scratch = dict(
        a_ref=bf(D.chains, D.sites, WIDTH),
        out_v=bf(N, D.chains, D.csites, WIDTH),
        w_buf=bf(7, WIDTH, WIDTH),
        xn=bf(D.rows, WIDTH),
        qkv_s=bf(3, D.hx, D.nx, D.sites, L),
        kv_r=bf(2, H, sites, L),
        q_r=bf(N, H, D.prows, L),
        l_own=f32(N, H, D.half, sites),
        l_send=bf(N, H, D.half, sites),
        l_recv=bf(N, H, D.half, sites),
        y_send=bf(N, H, D.half, sites),
        y_recv=bf(N, H, D.ny, D.yrows, sites),
        z_send=bf(N, H, D.yrows * sites // LANES, LANES),
        z_recv=bf(N, H, D.yrows * sites // LANES, LANES),
        p_send=bf(N, H, D.zrows * sites // LANES, LANES),
        p_z=bf(N, H, D.yrows * sites // LANES, LANES),
        p_full=bf(N, H, D.prows, sites),
        o_send=bf(N, H, D.prows, L),
        m_recv=bf(N, 2, H, D.nx, D.csites, L),
        wo_buf=bf(H, D.nx, HEAD, WIDTH),
        acc=f32(N, D.col_len, WIDTH),
        a_res=bf(N, 2, D.chains, D.csites, WIDTH),
        mix=bf(D.pair * D.csites, L),
        c_f32=f32(SLABS, D.col_len, LANES),
        c_send=bf(N, 2 * D.col_len, WIDTH // 2),
        c_recv=bf(N, 2 * D.col_len, WIDTH // 2),
        wide_buf=f32(D.col_len, WIDTH),
        cn=bf(D.col_len, WIDTH),
        c_qkv=bf(3, D.col_len, WIDTH),
        c_mix=bf(D.col_len, WIDTH),
        r_send=bf(N, 2 * D.col_len, WIDTH // 2),
        r_recv=bf(N, 2 * D.col_len, WIDTH // 2),
        f_send=bf(N, D.chains, D.csites, WIDTH),
        w_sem=sem(7), wo_sem=sem(H),
        x_ss=sem((2 + N) * H), x_rs=sem((2 + N) * H), x_ls=sem((2 + N) * H),
        a_ls=sem(N), a_ss=sem(N), a_rs=sem(N),
        c_ss=sem(N, H), c_rs=sem(N, H), y_ss=sem(N, H), y_rs=sem(N, H), z_ss=sem(N, H), z_rs=sem(N, H),
        pz_ss=sem(N, H), pz_rs=sem(N, H), py_ss=sem(N, H), py_rs=sem(N, H), pc_ss=sem(N, H), pc_rs=sem(N, H),
        o_ss=sem(N, H), o_rs=sem(N, H), o_ls=sem(N, H),
        i_ss=sem(N), i_rs=sem(N), i_ls=sem(N), b_ss=sem(N), b_rs=sem(N), b_ls=sem(N),
        f_ss=sem(N), f_rs=sem(N), out_sem=sem(N + 1),
    )
    flops = 2 * (8 * D.rows * WIDTH * WIDTH + 2 * D.hx * sites * sites * L)
    return pl.pallas_call(
        functools.partial(layer, D),
        out_shape=jax.ShapeDtypeStruct(a.shape, a.dtype),
        in_specs=[hbm] + [vmem] * 2 + [hbm] * 8,
        out_specs=hbm,
        scratch_shapes=list(scratch.values()),
        compiler_params=pltpu.CompilerParams(
            collective_id=0, has_side_effects=True, vmem_limit_bytes=60 * 2**20
        ),
        cost_estimate=pl.CostEstimate(flops=flops, bytes_accessed=12 * 2**20, transcendentals=2**21),
        name="msa_layer",
    )(a, g1, g2, wq, wk, wv, wo.reshape(D.nx, H, HEAD, WIDTH), cq, ck, cv, co)


def solution(mesh):
    nseq, nx = mesh.shape["seq"], mesh.shape["res"]
    ny = 4

    def step(a, *rest):
        D = Dims(nseq, nx, ny, a.shape[0], a.shape[1])
        return on_device(D, a, *rest)

    in_specs = (P("seq", "res", None),) + (P(),) * 10
    return jax.shard_map(
        step, mesh=mesh, in_specs=in_specs, out_specs=P("seq", "res", None), check_vma=False
    )
```
